32 devices in a mesh: srv: 16 (over z, y, x), head: 2 (over core).
Axes of the slice: x: 2, y: 2, z: 4, core: 2. Of those that a mesh axis runs over, the one named last changes fastest.
Arguments:
- tokens: bfloat16 [4096, 4096], P(('srv', 'head')), may hold values from -10.5 to 10.5
- doc_ids: int32 [4096], P(('srv', 'head')), may hold values from 0 to 15, never falling along the last dimension, each value on 1 to 512 neighbouring positions
- w_query: bfloat16 [4096, 2048], P(None, 'head'), may hold values from -1 to 1
- w_key: bfloat16 [4096, 512], P(None, 'head'), may hold values from -1.5 to 1.5
- value_weight: bfloat16 [4096, 512], P(None, 'head'), may hold values from -0.09375 to 0.09375
Outputs:
- attended: bfloat16 [4096, 2048], P(('srv', 'head'))
The draws below stay inside these ranges and needn't reach their ends.
Inputs may be any that keep to these rules, and one draw needn't show every extreme that they name: `doc_ids`: documents are consecutive runs of at most 512 tokens; one has exactly that many.
All inputs are finite; a program needn't handle non-finite values.
Results may differ from the reference program's by a relative error of at most 0.012.
The reference program's roundings to bfloat16 on the way count: a program that leaves them out, or rounds other values in their place, can miss the bound.
Values may be sent and summed in bfloat16 or wider, within the bound.
A program may use at most 64 MiB of HBM per device.

```python
import math
import jax
import jax.numpy as jnp
import numpy as np
from jax import lax

MODEL_WIDTH = 4096
QUERY_HEADS = 16
KEY_VALUE_HEADS = 4
HEAD_SIZE = 128
SPAN = 2
TOK_DEV = 128
GROUP_TOK = 256
TOKENS = 4096
DOCS = 16
N_HEAD = 2


def shared_query(key):
    return jax.random.truncated_normal(key, -6.0, 6.0, (MODEL_WIDTH, QUERY_HEADS * HEAD_SIZE), jnp.float32) * MODEL_WIDTH ** (-0.5)


def draw_w_query(key, part):
    return shared_query(key).astype(jnp.bfloat16)


def draw_w_key(key, part):
    key = jax.random.fold_in(key, 7)
    local_portion = jax.random.truncated_normal(key, -6.0, 6.0, (MODEL_WIDTH, KEY_VALUE_HEADS * HEAD_SIZE), jnp.float32) * MODEL_WIDTH ** (-0.5)
    return local_portion.astype(jnp.bfloat16)


def draw_tokens(key, part):
    key = jax.random.fold_in(key, 3)
    entry_key = jax.random.fold_in(key, 0)
    return jax.random.truncated_normal(entry_key, -6.0, 6.0, (TOKENS, MODEL_WIDTH), jnp.float32).astype(jnp.bfloat16)


def level_of(stream_key, dims, cuts, smallest, high):
    def one(dim, shards_of):
        heights = jax.random.uniform(jax.random.fold_in(jax.random.fold_in(stream_key, 6), dim), (shards_of,), jnp.float32, smallest / len(cuts), high / len(cuts))
        return jnp.repeat(jnp.exp(heights), dims[dim] // shards_of).reshape((-1,) + (1,) * (len(dims) - dim - 1))

    gain = one(*cuts[0])
    for cut in cuts[1:]:
        gain = gain * one(*cut)
    return gain


def profile(amount, total, reach, slope):
    loads = [(1 << 20) // math.isqrt(rank ** slope) + 1 for rank in range(2, amount + 1)]
    rest, holding = total - reach - (amount - 1), [1] * (amount - 1)
    while rest > 0:
        movable = [i for i in range(amount - 1) if holding[i] < reach]
        whole, remaining = sum([loads[i] for i in movable]), rest
        for i in movable:
            extra = min(reach - holding[i], max(1, remaining * loads[i] // whole), rest)
            holding[i] = holding[i] + extra
            rest = rest - extra
    return np.array([reach] + holding)


def ragged_sizes(key, number_of, total, reach, lean):
    if number_of == 2:
        one = jax.random.randint(key, (), max(1, total - reach), min(reach, total - 1) + 1)
        return jnp.stack([one, total - one])
    lengths = jnp.asarray(profile(number_of, total, reach, lean), jnp.int32)
    pairs = (number_of - 1) // 2
    source_of, taker = lengths[1:1 + 2 * pairs:2], lengths[2:2 + 2 * pairs:2]
    room = jnp.minimum(source_of - 1, reach - taker)
    shifted = jax.random.randint(jax.random.fold_in(key, 1), (pairs,), 0, 1 << 20) % (room + 1)
    lengths = lengths.at[1:1 + 2 * pairs:2].set(source_of - shifted).at[2:2 + 2 * pairs:2].set(taker + shifted)
    return lengths[jax.random.permutation(jax.random.fold_in(key, 2), number_of)]


def gaussian(own_key, shape, width, bound, pieces=(), kind=jnp.bfloat16):
    values = width * jax.random.normal(own_key, shape, jnp.float32)
    if pieces:
        values = values * level_of(own_key, shape, pieces, -0.22, 0.18)
    return jnp.clip(values, -bound, bound).astype(kind)


def setup_inputs(seed: int = 0) -> dict:
    seeds = jax.random.split(jax.random.key(seed), 6)
    tokens = draw_tokens(jax.random.fold_in(seeds[5], 71), 0)
    doc_ids = jnp.searchsorted(jnp.cumsum(ragged_sizes(seeds[1], DOCS, TOKENS, SPAN * GROUP_TOK, 2)), jnp.arange(TOKENS), side="right").astype(jnp.int32)
    w_query = draw_w_query(jax.random.fold_in(seeds[5], 71), 0)
    w_key = draw_w_key(jax.random.fold_in(seeds[5], 71), 0)
    value_weight = gaussian(seeds[4], (MODEL_WIDTH, KEY_VALUE_HEADS * HEAD_SIZE), MODEL_WIDTH ** -0.5, 0.09375, ((1, 2),))
    return dict(tokens=tokens, doc_ids=doc_ids, w_query=w_query, w_key=w_key, value_weight=value_weight)


def reference(tokens, doc_ids, w_query, w_key, value_weight):
    group_token = TOK_DEV * N_HEAD
    groups = TOKENS // group_token
    repeat_factor = QUERY_HEADS // KEY_VALUE_HEADS
    query_row_set = jnp.dot(tokens, w_query, preferred_element_type=jnp.float32).astype(jnp.bfloat16)
    key_matrix_rows = jnp.dot(tokens, w_key, preferred_element_type=jnp.float32).astype(jnp.bfloat16)
    value_matrix_rows = jnp.dot(tokens, value_weight, preferred_element_type=jnp.float32).astype(jnp.bfloat16)
    leading_padding = SPAN * group_token
    key_padding = jnp.concatenate([jnp.zeros((leading_padding, KEY_VALUE_HEADS * HEAD_SIZE), jnp.bfloat16), key_matrix_rows], 0)
    value_padding = jnp.concatenate([jnp.zeros((leading_padding, KEY_VALUE_HEADS * HEAD_SIZE), jnp.bfloat16), value_matrix_rows], 0)
    doc_index = doc_ids.astype(jnp.int32)
    doc_pad = jnp.concatenate([jnp.full((leading_padding,), -1, jnp.int32), doc_index], 0)
    key_span_width = (SPAN + 1) * group_token
    logit_scale = 1.0 / (HEAD_SIZE ** 0.5)

    def one_group(group_index):
        starting_row = (group_index * group_token).astype(jnp.int32)
        query_matrix = lax.dynamic_slice_in_dim(query_row_set, starting_row, group_token, 0).reshape(group_token, KEY_VALUE_HEADS, repeat_factor, HEAD_SIZE)
        key_frame = lax.dynamic_slice_in_dim(key_padding, starting_row, key_span_width, 0).reshape(key_span_width, KEY_VALUE_HEADS, HEAD_SIZE)
        value_frame = lax.dynamic_slice_in_dim(value_padding, starting_row, key_span_width, 0).reshape(key_span_width, KEY_VALUE_HEADS, HEAD_SIZE)
        query_doc = lax.dynamic_slice_in_dim(doc_index, starting_row, group_token, 0)
        key_doc = lax.dynamic_slice_in_dim(doc_pad, starting_row, key_span_width, 0)
        query_pos = starting_row + jnp.arange(group_token, dtype=jnp.int32)
        key_pos = starting_row - leading_padding + jnp.arange(key_span_width, dtype=jnp.int32)
        allowed = (query_doc[:, None] == key_doc[None, :]) & (key_pos[None, :] <= query_pos[:, None]) & (key_pos[None, :] >= 0)
        score_matrix = jnp.einsum("hfwl,afl->fwha", query_matrix.astype(jnp.float32), key_frame.astype(jnp.float32)) * logit_scale
        score_matrix = jnp.where(allowed[None, None], score_matrix, -1e30)
        row_max = jnp.max(score_matrix, -1, keepdims=True)
        exponent = jnp.exp(score_matrix - row_max)
        row_total = jnp.sum(exponent, -1)
        attention_weight = exponent.astype(jnp.bfloat16)
        summed_output = jnp.einsum("mjwh,hmn->mjwn", attention_weight.astype(jnp.float32), value_frame.astype(jnp.float32))
        result = summed_output / row_total[..., None]
        return jnp.transpose(result, (2, 0, 1, 3)).reshape(group_token, QUERY_HEADS * HEAD_SIZE).astype(jnp.bfloat16)

    attended = lax.map(one_group, jnp.arange(groups, dtype=jnp.int32)).reshape(TOKENS, QUERY_HEADS * HEAD_SIZE)
    return attended
```

```python
import functools
import math

import jax
import jax.numpy as jnp
from jax import lax
from jax.experimental import pallas as pl
from jax.experimental.pallas import tpu as pltpu
from jax.sharding import PartitionSpec as P

HEAD = 128
REPEAT = 4
EXP2_SCALE = math.log2(math.e) / math.sqrt(HEAD)
MASKED = -1e30
MESH = pl.DeviceIdType.MESH


def kernel(
    n,
    tok_hbm,
    doc_hbm,
    wq_hbm,
    wk_hbm,
    wv_hbm,
    out_ref,
    tok,
    wkv,
    wq,
    kv,
    q,
    acc,
    top,
    bias,
    docs,
    stage,
    tok_sem,
    wkv_sem,
    wq_sem,
    doc_sem,
    pair_send,
    pair_recv,
    doc_send,
    doc_recv,
    kv_send,
    kv_recv,
    out_send,
    out_recv,
):
    srv = lax.axis_index("srv")
    head = lax.axis_index("head")
    other = 1 - head
    tok_dev = tok.shape[1]
    kv_heads = wkv.shape[0]
    q_blocks = wq.shape[0]
    even = srv % 2 == 0
    odd = srv % 2 == 1

    def local(src, dst, sem):
        return pltpu.make_async_copy(src, dst, sem)

    own_tok = local(tok_hbm, tok.at[head], tok_sem)
    own_doc = local(doc_hbm, docs.at[head], doc_sem)
    wkv_copies = []
    for c in range(kv_heads):
        cols = pl.ds(c * HEAD, HEAD)
        wkv_copies.append(
            (
                local(wk_hbm.at[:, cols], wkv.at[c, :, pl.ds(0, HEAD)], wkv_sem.at[c, 0]),
                local(wv_hbm.at[:, cols], wkv.at[c, :, pl.ds(HEAD, HEAD)], wkv_sem.at[c, 1]),
            )
        )
    wq_copies = [
        local(wq_hbm.at[:, pl.ds(j * 256, 256)], wq.at[j], wq_sem.at[j]) for j in range(q_blocks)
    ]
    own_tok.start()
    own_doc.start()
    for pair in wkv_copies:
        for copy in pair:
            copy.start()

    barrier = pltpu.get_barrier_semaphore()
    pl.semaphore_signal(barrier, inc=1, device_id=(srv, other), device_id_type=MESH)
    count = jnp.int32(1)
    for by in (-2, -1, 1, 2):
        there = (srv + by >= 0) & (srv + by < n)
        count = count + there.astype(jnp.int32)

        @pl.when(there)
        def _(by=by):
            pl.semaphore_signal(barrier, inc=1, device_id=(srv + by, head), device_id_type=MESH)

    pl.semaphore_wait(barrier, count)

    def remote(src, dst, send, recv, device):
        return pltpu.make_async_remote_copy(
            src_ref=src,
            dst_ref=dst,
            send_sem=send,
            recv_sem=recv,
            device_id=device,
            device_id_type=MESH,
        )

    partner = (srv, other)
    pair_tok = remote(tok_hbm, tok.at[head], pair_send.at[0], pair_recv.at[0], partner)
    pair_doc = remote(doc_hbm, docs.at[head], pair_send.at[1], pair_recv.at[1], partner)
    pair_doc.start()
    pair_tok.start()
    for copy in wq_copies:
        copy.start()

    def doc_copy(by):
        return remote(
            docs.at[pl.ds(0, 2)],
            docs.at[pl.ds(2 * by, 2)],
            doc_send.at[by - 1],
            doc_recv.at[by - 1],
            (srv + by, head),
        )

    halves = (head, other)

    def kv_copy(by, turn, c):
        return remote(
            kv.at[0, c, halves[turn]],
            kv.at[by, c, halves[turn]],
            kv_send.at[by - 1, turn, c],
            kv_recv.at[by - 1, turn, c],
            (srv + by, head),
        )

    def kv_forward(turn, c):
        return remote(
            kv.at[2, c, halves[turn]],
            kv.at[1, c, halves[turn]],
            kv_send.at[0, turn, c],
            kv_recv.at[0, turn, c],
            (srv - 1, head),
        )

    sends_one = even & (srv + 1 < n)
    sends_two = srv + 2 < n
    forwards = odd & (srv >= 2)

    def project_kv(turn, c):
        kv[0, c, halves[turn]] = jnp.dot(
            tok[halves[turn]], wkv[c], preferred_element_type=jnp.float32
        ).astype(jnp.bfloat16)

        @pl.when(sends_two)
        def _():
            kv_copy(2, turn, c).start()

        @pl.when(sends_one)
        def _():
            kv_copy(1, turn, c).start()

    def project_q(turn, j):
        block = jnp.dot(
            tok[halves[turn]], wq[j], preferred_element_type=jnp.float32
        ).astype(jnp.bfloat16)
        q[2 * j, halves[turn]] = block[:, :HEAD]
        q[2 * j + 1, halves[turn]] = block[:, HEAD:]

    def forward(turn, c):
        @pl.when(forwards)
        def _():
            kv_copy(2, turn, c).wait_recv()
            kv_forward(turn, c).start()

    own_tok.wait()
    own_doc.wait()
    for c in range(kv_heads):
        for copy in wkv_copies[c]:
            copy.wait()
        project_kv(0, c)
    pair_doc.wait_recv()
    for by in (1, 2):

        @pl.when(srv + by < n)
        def _(by=by):
            doc_copy(by).start()

    for j in range(q_blocks):
        wq_copies[j].wait()
        project_q(0, j)
    pair_tok.wait_recv()
    for c in range(kv_heads):
        project_kv(1, c)
    for c in range(kv_heads):
        forward(0, c)
    for j in range(q_blocks):
        project_q(1, j)

    def column(part):
        ids = docs[part].astype(jnp.float32)
        return jnp.transpose(jnp.broadcast_to(ids, (HEAD, HEAD)))

    def set_bias(block):
        for r in range(2):
            mine = column(r)
            for s in range(2):
                theirs = docs[2 * block + s].astype(jnp.float32)
                allowed = mine == theirs
                if block == 0:
                    rows = lax.broadcasted_iota(jnp.int32, (HEAD, HEAD), 0) + r * HEAD
                    cols = lax.broadcasted_iota(jnp.int32, (HEAD, HEAD), 1) + s * HEAD
                    allowed = allowed & (cols <= rows)
                bias[block, r, :, s * HEAD : (s + 1) * HEAD] = jnp.where(allowed, 0.0, MASKED)

    ones = jnp.ones((2 * tok_dev, HEAD), jnp.bfloat16)

    def attend(block, c):
        both = kv[block, c].reshape(2 * tok_dev, 2 * HEAD)
        keys = both[:, :HEAD]
        values = jnp.concatenate([both[:, HEAD:], ones], axis=1)
        for g in range(REPEAT):
            h = c * REPEAT + g
            for r in range(2):
                score = lax.dot_general(
                    q[h, r], keys, (((1,), (1,)), ((), ())), preferred_element_type=jnp.float32
                )
                score = score + bias[block, r]
                high = jnp.max(score, axis=1, keepdims=True)
                if block:
                    before = top[h, r][:, :1]
                    high = jnp.maximum(high, before)
                weight = jnp.exp2((score - high) * EXP2_SCALE).astype(jnp.bfloat16)
                part = jnp.dot(weight, values, preferred_element_type=jnp.float32)
                if block:
                    part = part + acc[h, r] * jnp.exp2((before - high) * EXP2_SCALE)
                acc[h, r] = part
                if block != 1:
                    top[h, r] = jnp.broadcast_to(high, (tok_dev, HEAD))

    set_bias(0)
    for c in range(kv_heads):
        attend(0, c)
    for c in range(kv_heads):
        forward(1, c)

    @pl.when(srv >= 2)
    def _():
        doc_copy(2).wait_recv()
        set_bias(2)
        for c in range(kv_heads):

            @pl.when(even)
            def _():
                for turn in range(2):
                    kv_copy(2, turn, c).wait_recv()

            attend(2, c)

    @pl.when(srv >= 1)
    def _():
        doc_copy(1).wait_recv()
        set_bias(1)

    def out_copy(c):
        width = REPEAT * HEAD
        column_of = pl.multiple_of(head * kv_heads * width + c * width, width)
        return remote(
            stage.at[c],
            out_ref.at[:, pl.ds(column_of, width)],
            out_send.at[c],
            out_recv.at[c],
            partner,
        )

    for c in range(kv_heads):

        @pl.when(srv >= 1)
        def _():
            for turn in range(2):
                kv_copy(1, turn, c).wait_recv()
            attend(1, c)

        for g in range(REPEAT):
            h = c * REPEAT + g
            theirs = acc[h, other]
            stage[c, :, g * HEAD : (g + 1) * HEAD] = (theirs[:, :HEAD] / theirs[:, HEAD:]).astype(
                jnp.bfloat16
            )
        out_copy(c).start()
        for g in range(REPEAT):
            h = c * REPEAT + g
            mine = acc[h, head]
            at = pl.multiple_of((head * kv_heads + c) * REPEAT * HEAD + g * HEAD, HEAD)
            out_ref[:, pl.ds(at, HEAD)] = (mine[:, :HEAD] / mine[:, HEAD:]).astype(jnp.bfloat16)

    pair_tok.wait_send()
    pair_doc.wait_send()
    for by in (1, 2):

        @pl.when(srv + by < n)
        def _(by=by):
            doc_copy(by).wait_send()

    for turn in range(2):
        for c in range(kv_heads):

            @pl.when(sends_two)
            def _():
                kv_copy(2, turn, c).wait_send()

            @pl.when(sends_one)
            def _():
                kv_copy(1, turn, c).wait_send()

            @pl.when(forwards)
            def _():
                kv_forward(turn, c).wait_send()

    for c in range(kv_heads):
        out_copy(c).wait()


def on_device(n, tokens, doc_ids, w_query, w_key, value_weight):
    tok_dev, width = tokens.shape
    kv_heads = w_key.shape[1] // HEAD
    heads = w_query.shape[1] // HEAD
    q_blocks = heads // 2
    bf16, f32 = jnp.bfloat16, jnp.float32
    dma = pltpu.SemaphoreType.DMA
    return pl.pallas_call(
        functools.partial(kernel, n),
        out_shape=jax.ShapeDtypeStruct((tok_dev, 2 * heads * HEAD), bf16),
        in_specs=[pl.BlockSpec(memory_space=pl.ANY)] * 5,
        out_specs=pl.BlockSpec(memory_space=pltpu.VMEM),
        scratch_shapes=[
            pltpu.VMEM((2, tok_dev, width), bf16),
            pltpu.VMEM((kv_heads, width, 2 * HEAD), bf16),
            pltpu.VMEM((q_blocks, width, 2 * HEAD), bf16),
            pltpu.VMEM((3, kv_heads, 2, tok_dev, 2 * HEAD), bf16),
            pltpu.VMEM((heads, 2, tok_dev, HEAD), bf16),
            pltpu.VMEM((heads, 2, tok_dev, 2 * HEAD), f32),
            pltpu.VMEM((heads, 2, tok_dev, HEAD), f32),
            pltpu.VMEM((3, 2, tok_dev, 2 * tok_dev), f32),
            pltpu.VMEM((6, 1, tok_dev), jnp.int32),
            pltpu.VMEM((kv_heads, tok_dev, REPEAT * HEAD), bf16),
            dma,
            dma((kv_heads, 2)),
            dma((q_blocks,)),
            dma,
            dma((2,)),
            dma((2,)),
            dma((2,)),
            dma((2,)),
            dma((2, 2, kv_heads)),
            dma((2, 2, kv_heads)),
            dma((kv_heads,)),
            dma((kv_heads,)),
        ],
        compiler_params=pltpu.CompilerParams(
            collective_id=0, has_side_effects=True, vmem_limit_bytes=48 * 1024 * 1024
        ),
    )(tokens, doc_ids.reshape(1, tok_dev), w_query, w_key, value_weight)


def solution(mesh):
    in_specs = (
        P(("srv", "head"), None),
        P(("srv", "head")),
        P(None, "head"),
        P(None, "head"),
        P(None, "head"),
    )
    return jax.shard_map(
        functools.partial(on_device, mesh.shape["srv"]),
        mesh=mesh,
        in_specs=in_specs,
        out_specs=P(("srv", "head"), None),
        check_vma=False,
    )
```

```python
import functools
import math

import jax
import jax.numpy as jnp
from jax import lax
from jax.experimental import pallas as pl
from jax.experimental.pallas import tpu as pltpu
from jax.sharding import PartitionSpec as P

HEAD = 128
REPEAT = 4
EXP2_SCALE = math.log2(math.e) / math.sqrt(HEAD)
MASKED = -1e30
MESH = pl.DeviceIdType.MESH


def kernel(
    n,
    tok_hbm,
    doc_hbm,
    wq_hbm,
    wk_hbm,
    wv_hbm,
    out_ref,
    tok,
    wkv,
    wq,
    kv,
    q,
    acc,
    top,
    bias,
    docs,
    stage,
    tok_sem,
    wkv_sem,
    wq_sem,
    doc_sem,
    pair_send,
    pair_recv,
    doc_send,
    doc_recv,
    kv_send,
    kv_recv,
    out_send,
    out_recv,
):
    srv = lax.axis_index("srv")
    head = lax.axis_index("head")
    other = 1 - head
    tok_dev = tok.shape[1]
    kv_heads = wkv.shape[0]
    q_blocks = wq.shape[0]
    even = srv % 2 == 0
    odd = srv % 2 == 1

    def local(src, dst, sem):
        return pltpu.make_async_copy(src, dst, sem)

    own_tok = local(tok_hbm, tok.at[head], tok_sem)
    own_doc = local(doc_hbm, docs.at[head], doc_sem)
    wkv_copies = []
    for c in range(kv_heads):
        cols = pl.ds(c * HEAD, HEAD)
        wkv_copies.append(
            (
                local(wk_hbm.at[:, cols], wkv.at[c, :, pl.ds(0, HEAD)], wkv_sem.at[c, 0]),
                local(wv_hbm.at[:, cols], wkv.at[c, :, pl.ds(HEAD, HEAD)], wkv_sem.at[c, 1]),
            )
        )
    wq_copies = [
        local(wq_hbm.at[:, pl.ds(j * 256, 256)], wq.at[j], wq_sem.at[j]) for j in range(q_blocks)
    ]
    own_tok.start()
    own_doc.start()
    for pair in wkv_copies:
        for copy in pair:
            copy.start()
    for copy in wq_copies:
        copy.start()

    barrier = pltpu.get_barrier_semaphore()
    pl.semaphore_signal(barrier, inc=1, device_id=(srv, other), device_id_type=MESH)
    count = jnp.int32(1)
    for by in (-2, -1, 1, 2):
        there = (srv + by >= 0) & (srv + by < n)
        count = count + there.astype(jnp.int32)

        @pl.when(there)
        def _(by=by):
            pl.semaphore_signal(barrier, inc=1, device_id=(srv + by, head), device_id_type=MESH)

    pl.semaphore_wait(barrier, count)

    def remote(src, dst, send, recv, device):
        return pltpu.make_async_remote_copy(
            src_ref=src,
            dst_ref=dst,
            send_sem=send,
            recv_sem=recv,
            device_id=device,
            device_id_type=MESH,
        )

    partner = (srv, other)
    pair_tok = remote(tok_hbm, tok.at[head], pair_send.at[0], pair_recv.at[0], partner)
    pair_doc = remote(doc_hbm, docs.at[head], pair_send.at[1], pair_recv.at[1], partner)
    pair_doc.start()
    pair_tok.start()

    def doc_copy(by):
        return remote(
            docs.at[pl.ds(0, 2)],
            docs.at[pl.ds(2 * by, 2)],
            doc_send.at[by - 1],
            doc_recv.at[by - 1],
            (srv + by, head),
        )

    halves = (head, other)

    def kv_copy(by, turn, c):
        return remote(
            kv.at[0, c, halves[turn]],
            kv.at[by, c, halves[turn]],
            kv_send.at[by - 1, turn, c],
            kv_recv.at[by - 1, turn, c],
            (srv + by, head),
        )

    def kv_forward(turn, c):
        return remote(
            kv.at[2, c, halves[turn]],
            kv.at[1, c, halves[turn]],
            kv_send.at[0, turn, c],
            kv_recv.at[0, turn, c],
            (srv - 1, head),
        )

    sends_one = even & (srv + 1 < n)
    sends_two = srv + 2 < n
    forwards = odd & (srv >= 2)

    def project_kv(turn, c):
        kv[0, c, halves[turn]] = jnp.dot(
            tok[halves[turn]], wkv[c], preferred_element_type=jnp.float32
        ).astype(jnp.bfloat16)

        @pl.when(sends_two)
        def _():
            kv_copy(2, turn, c).start()

        @pl.when(sends_one)
        def _():
            kv_copy(1, turn, c).start()

    def project_q(j):
        block = jnp.dot(
            tok[...].reshape(2 * tok_dev, tok.shape[2]), wq[j], preferred_element_type=jnp.float32
        ).astype(jnp.bfloat16)
        q[2 * j] = block[:, :HEAD]
        q[2 * j + 1] = block[:, HEAD:]

    def forward(turn, c):
        @pl.when(forwards)
        def _():
            kv_copy(2, turn, c).wait_recv()
            kv_forward(turn, c).start()

    own_tok.wait()
    own_doc.wait()
    for c in range(kv_heads):
        for copy in wkv_copies[c]:
            copy.wait()
        project_kv(0, c)
    pair_doc.wait_recv()
    for by in (1, 2):

        @pl.when(srv + by < n)
        def _(by=by):
            doc_copy(by).start()

    pair_tok.wait_recv()
    for c in range(kv_heads):
        project_kv(1, c)
    for j in range(q_blocks):
        if j == q_blocks // 2:
            for c in range(kv_heads):
                forward(0, c)
        wq_copies[j].wait()
        project_q(j)

    def column(part):
        ids = docs[part].astype(jnp.float32)
        return jnp.transpose(jnp.broadcast_to(ids, (HEAD, HEAD)))

    def set_bias(block):
        for r in range(2):
            mine = column(r)
            for s in range(2):
                theirs = docs[2 * block + s].astype(jnp.float32)
                allowed = mine == theirs
                if block == 0:
                    rows = lax.broadcasted_iota(jnp.int32, (HEAD, HEAD), 0) + r * HEAD
                    cols = lax.broadcasted_iota(jnp.int32, (HEAD, HEAD), 1) + s * HEAD
                    allowed = allowed & (cols <= rows)
                bias[block, r * HEAD : (r + 1) * HEAD, s * HEAD : (s + 1) * HEAD] = jnp.where(allowed, 0.0, MASKED)

    ones = jnp.ones((2 * tok_dev, HEAD), jnp.bfloat16)

    def attend(block, c):
        both = kv[block, c].reshape(2 * tok_dev, 2 * HEAD)
        keys = both[:, :HEAD]
        values = jnp.concatenate([both[:, HEAD:], ones], axis=1)

        def scores(g):
            return lax.dot_general(
                q[c * REPEAT + g],
                keys,
                (((1,), (1,)), ((), ())),
                preferred_element_type=jnp.float32,
            )

        ahead = scores(0)
        for g in range(REPEAT):
            h = c * REPEAT + g
            score = ahead + bias[block]
            if g + 1 < REPEAT:
                ahead = scores(g + 1)
            high = jnp.max(score, axis=1, keepdims=True)
            if block:
                before = top[h][:, :1]
                high = jnp.maximum(high, before)
            weight = jnp.exp2((score - high) * EXP2_SCALE).astype(jnp.bfloat16)
            part = jnp.dot(weight, values, preferred_element_type=jnp.float32)
            if block:
                part = part + acc[h] * jnp.exp2((before - high) * EXP2_SCALE)
            acc[h] = part
            if block != 1:
                top[h] = jnp.broadcast_to(high, (2 * tok_dev, HEAD))

    set_bias(0)
    for c in range(kv_heads):
        attend(0, c)
    for c in range(kv_heads):
        forward(1, c)

    @pl.when(srv >= 2)
    def _():
        doc_copy(2).wait_recv()
        set_bias(2)
        for c in range(kv_heads):

            @pl.when(even)
            def _():
                for turn in range(2):
                    kv_copy(2, turn, c).wait_recv()

            attend(2, c)

    @pl.when(srv >= 1)
    def _():
        doc_copy(1).wait_recv()
        set_bias(1)

    def out_copy(c):
        width = REPEAT * HEAD
        column_of = pl.multiple_of(head * kv_heads * width + c * width, width)
        return remote(
            stage.at[c],
            out_ref.at[:, pl.ds(column_of, width)],
            out_send.at[c],
            out_recv.at[c],
            partner,
        )

    for c in range(kv_heads):

        @pl.when(srv >= 1)
        def _():
            for turn in range(2):
                kv_copy(1, turn, c).wait_recv()
            attend(1, c)

        for g in range(REPEAT):
            h = c * REPEAT + g
            theirs = acc[h, pl.ds(pl.multiple_of(other * tok_dev, tok_dev), tok_dev)]
            stage[c, :, g * HEAD : (g + 1) * HEAD] = (theirs[:, :HEAD] / theirs[:, HEAD:]).astype(
                jnp.bfloat16
            )
        out_copy(c).start()
        for g in range(REPEAT):
            h = c * REPEAT + g
            mine = acc[h, pl.ds(pl.multiple_of(head * tok_dev, tok_dev), tok_dev)]
            at = pl.multiple_of((head * kv_heads + c) * REPEAT * HEAD + g * HEAD, HEAD)
            out_ref[:, pl.ds(at, HEAD)] = (mine[:, :HEAD] / mine[:, HEAD:]).astype(jnp.bfloat16)

    pair_tok.wait_send()
    pair_doc.wait_send()
    for by in (1, 2):

        @pl.when(srv + by < n)
        def _(by=by):
            doc_copy(by).wait_send()

    for turn in range(2):
        for c in range(kv_heads):

            @pl.when(sends_two)
            def _():
                kv_copy(2, turn, c).wait_send()

            @pl.when(sends_one)
            def _():
                kv_copy(1, turn, c).wait_send()

            @pl.when(forwards)
            def _():
                kv_forward(turn, c).wait_send()

    for c in range(kv_heads):
        out_copy(c).wait()


def on_device(n, tokens, doc_ids, w_query, w_key, value_weight):
    tok_dev, width = tokens.shape
    kv_heads = w_key.shape[1] // HEAD
    heads = w_query.shape[1] // HEAD
    q_blocks = heads // 2
    bf16, f32 = jnp.bfloat16, jnp.float32
    dma = pltpu.SemaphoreType.DMA
    return pl.pallas_call(
        functools.partial(kernel, n),
        out_shape=jax.ShapeDtypeStruct((tok_dev, 2 * heads * HEAD), bf16),
        in_specs=[pl.BlockSpec(memory_space=pltpu.HBM)] * 5,
        out_specs=pl.BlockSpec(memory_space=pltpu.VMEM),
        scratch_shapes=[
            pltpu.VMEM((2, tok_dev, width), bf16),
            pltpu.VMEM((kv_heads, width, 2 * HEAD), bf16),
            pltpu.VMEM((q_blocks, width, 2 * HEAD), bf16),
            pltpu.VMEM((3, kv_heads, 2, tok_dev, 2 * HEAD), bf16),
            pltpu.VMEM((heads, 2 * tok_dev, HEAD), bf16),
            pltpu.VMEM((heads, 2 * tok_dev, 2 * HEAD), f32),
            pltpu.VMEM((heads, 2 * tok_dev, HEAD), f32),
            pltpu.VMEM((3, 2 * tok_dev, 2 * tok_dev), f32),
            pltpu.VMEM((6, 1, tok_dev), jnp.int32),
            pltpu.VMEM((kv_heads, tok_dev, REPEAT * HEAD), bf16),
            dma,
            dma((kv_heads, 2)),
            dma((q_blocks,)),
            dma,
            dma((2,)),
            dma((2,)),
            dma((2,)),
            dma((2,)),
            dma((2, 2, kv_heads)),
            dma((2, 2, kv_heads)),
            dma((kv_heads,)),
            dma((kv_heads,)),
        ],
        compiler_params=pltpu.CompilerParams(
            collective_id=0, has_side_effects=True, vmem_limit_bytes=56 * 1024 * 1024
        ),
    )(tokens, doc_ids.reshape(1, tok_dev), w_query, w_key, value_weight)


def solution(mesh):
    in_specs = (
        P(("srv", "head"), None),
        P(("srv", "head")),
        P(None, "head"),
        P(None, "head"),
        P(None, "head"),
    )
    return jax.shard_map(
        functools.partial(on_device, mesh.shape["srv"]),
        mesh=mesh,
        in_specs=in_specs,
        out_specs=P(("srv", "head"), None),
        check_vma=False,
    )
```

```python
import functools
import math

import jax
import jax.numpy as jnp
from jax import lax
from jax.experimental import pallas as pl
from jax.experimental.pallas import tpu as pltpu
from jax.sharding import PartitionSpec as P

HEAD = 128
REPEAT = 4
EXP2_SCALE = math.log2(math.e) / math.sqrt(HEAD)
MASKED = -1e30
ONES = 16
MESH = pl.DeviceIdType.MESH


def kernel(
    n,
    tok_hbm,
    doc_hbm,
    wq_hbm,
    wk_hbm,
    wv_hbm,
    out_ref,
    tok,
    wkv,
    wq,
    kv,
    q,
    acc,
    top,
    bias,
    docs,
    stage,
    tok_sem,
    wkv_sem,
    wq_sem,
    doc_sem,
    pair_send,
    pair_recv,
    doc_send,
    doc_recv,
    kv_send,
    kv_recv,
    out_send,
    out_recv,
):
    srv = lax.axis_index("srv")
    head = lax.axis_index("head")
    other = 1 - head
    tok_dev = tok.shape[1]
    kv_heads = wkv.shape[0]
    q_blocks = wq.shape[0]
    even = srv % 2 == 0
    odd = srv % 2 == 1

    def local(src, dst, sem):
        return pltpu.make_async_copy(src, dst, sem)

    own_tok = local(tok_hbm, tok.at[head], tok_sem)
    own_doc = local(doc_hbm, docs.at[head], doc_sem)
    wkv_copies = []
    for c in range(kv_heads):
        cols = pl.ds(c * HEAD, HEAD)
        wkv_copies.append(
            (
                local(wk_hbm.at[:, cols], wkv.at[c, :, pl.ds(0, HEAD)], wkv_sem.at[c, 0]),
                local(wv_hbm.at[:, cols], wkv.at[c, :, pl.ds(HEAD, HEAD)], wkv_sem.at[c, 1]),
            )
        )
    wq_copies = [
        local(wq_hbm.at[:, pl.ds(j * 256, 256)], wq.at[j], wq_sem.at[j]) for j in range(q_blocks)
    ]
    own_tok.start()
    own_doc.start()
    for pair in wkv_copies:
        for copy in pair:
            copy.start()
    for copy in wq_copies:
        copy.start()

    barrier = pltpu.get_barrier_semaphore()
    pl.semaphore_signal(barrier, inc=1, device_id=(srv, other), device_id_type=MESH)
    count = jnp.int32(1)
    for by in (-2, -1, 1, 2):
        there = (srv + by >= 0) & (srv + by < n)
        count = count + there.astype(jnp.int32)

        @pl.when(there)
        def _(by=by):
            pl.semaphore_signal(barrier, inc=1, device_id=(srv + by, head), device_id_type=MESH)

    pl.semaphore_wait(barrier, count)

    def remote(src, dst, send, recv, device):
        return pltpu.make_async_remote_copy(
            src_ref=src,
            dst_ref=dst,
            send_sem=send,
            recv_sem=recv,
            device_id=device,
            device_id_type=MESH,
        )

    partner = (srv, other)
    pair_tok = remote(tok_hbm, tok.at[head], pair_send.at[0], pair_recv.at[0], partner)
    pair_doc = remote(doc_hbm, docs.at[head], pair_send.at[1], pair_recv.at[1], partner)
    pair_doc.start()
    pair_tok.start()

    def doc_copy(by):
        return remote(
            docs.at[pl.ds(0, 2)],
            docs.at[pl.ds(2 * by, 2)],
            doc_send.at[by - 1],
            doc_recv.at[by - 1],
            (srv + by, head),
        )

    halves = (head, other)

    def kv_copy(by, turn, c):
        return remote(
            kv.at[0, c, halves[turn]],
            kv.at[by, c, halves[turn]],
            kv_send.at[by - 1, turn, c],
            kv_recv.at[by - 1, turn, c],
            (srv + by, head),
        )

    def kv_forward(turn, c):
        return remote(
            kv.at[2, c, halves[turn]],
            kv.at[1, c, halves[turn]],
            kv_send.at[0, turn, c],
            kv_recv.at[0, turn, c],
            (srv - 1, head),
        )

    sends_one = even & (srv + 1 < n)
    sends_two = srv + 2 < n
    forwards = odd & (srv >= 2)

    def project_kv(turn, c):
        both = jnp.dot(tok[halves[turn]], wkv[c], preferred_element_type=jnp.float32)
        kv[0, c, halves[turn], :, :HEAD] = both[:, :HEAD].astype(jnp.bfloat16)
        kv[0, c, halves[turn], :, HEAD:] = jnp.transpose(both[:, HEAD:]).astype(jnp.bfloat16)

        @pl.when(sends_two)
        def _():
            kv_copy(2, turn, c).start()

        @pl.when(sends_one)
        def _():
            kv_copy(1, turn, c).start()

    def project_q(j):
        block = jnp.dot(
            tok[...].reshape(2 * tok_dev, tok.shape[2]), wq[j], preferred_element_type=jnp.float32
        ).astype(jnp.bfloat16)
        q[2 * j] = block[:, :HEAD]
        q[2 * j + 1] = block[:, HEAD:]

    def forward(turn, c):
        @pl.when(forwards)
        def _():
            kv_copy(2, turn, c).wait_recv()
            kv_forward(turn, c).start()

    own_tok.wait()
    own_doc.wait()
    for c in range(kv_heads):
        for copy in wkv_copies[c]:
            copy.wait()
        project_kv(0, c)
    pair_doc.wait_recv()
    for by in (1, 2):

        @pl.when(srv + by < n)
        def _(by=by):
            doc_copy(by).start()

    pair_tok.wait_recv()
    for c in range(kv_heads):
        project_kv(1, c)
    for j in range(q_blocks):
        if j == q_blocks // 2:
            for c in range(kv_heads):
                forward(0, c)
        wq_copies[j].wait()
        project_q(j)

    def column(part):
        ids = docs[part].astype(jnp.float32)
        return jnp.transpose(jnp.broadcast_to(ids, (HEAD, HEAD)))

    def set_bias(block):
        for s in range(2):
            theirs = column(2 * block + s)
            for r in range(2):
                mine = docs[r].astype(jnp.float32)
                allowed = theirs == mine
                if block == 0:
                    keys = lax.broadcasted_iota(jnp.int32, (HEAD, HEAD), 0) + s * HEAD
                    queries = lax.broadcasted_iota(jnp.int32, (HEAD, HEAD), 1) + r * HEAD
                    allowed = allowed & (keys <= queries)
                bias[block, r, s * HEAD : (s + 1) * HEAD, :] = jnp.where(allowed, 0.0, MASKED)

    first_key = {0: (0, 0), 1: (0, 0), 2: (0, tok_dev)}
    last_key = {0: (tok_dev, 2 * tok_dev), 1: (2 * tok_dev,) * 2, 2: (2 * tok_dev,) * 2}

    def attend(block, c):
        keys = kv[block, c].reshape(2 * tok_dev, 2 * HEAD)[:, :HEAD]
        values = jnp.concatenate([kv[block, c, 0, :, HEAD:], kv[block, c, 1, :, HEAD:]], axis=1)
        values = jnp.concatenate([values, jnp.ones((ONES, 2 * tok_dev), jnp.bfloat16)], axis=0)
        for g in range(REPEAT):
            h = c * REPEAT + g
            for r in range(2):
                lo, hi = first_key[block][r], last_key[block][r]
                score = lax.dot_general(
                    keys[lo:hi],
                    q[h, r * tok_dev : (r + 1) * tok_dev],
                    (((1,), (1,)), ((), ())),
                    preferred_element_type=jnp.float32,
                )
                score = score + bias[block, r, lo:hi]
                high = jnp.max(score, axis=0, keepdims=True)
                if block:
                    before = top[h, r]
                    high = jnp.maximum(high, before)
                weight = jnp.exp2((score - high) * EXP2_SCALE).astype(jnp.bfloat16)
                part = jnp.dot(values[:, lo:hi], weight, preferred_element_type=jnp.float32)
                if block:
                    part = part + acc[h, r] * jnp.exp2((before - high) * EXP2_SCALE)
                acc[h, r] = part
                if block != 1:
                    top[h, r] = high

    identity = (
        lax.broadcasted_iota(jnp.int32, (tok_dev, tok_dev), 0)
        == lax.broadcasted_iota(jnp.int32, (tok_dev, tok_dev), 1)
    ).astype(jnp.bfloat16)

    def result(h, half):
        total = acc[h, half, HEAD : HEAD + 1]
        rounded = (acc[h, half, :HEAD] * (1.0 / total)).astype(jnp.bfloat16)
        return lax.dot_general(
            identity, rounded, (((1,), (1,)), ((), ())), preferred_element_type=jnp.float32
        ).astype(jnp.bfloat16)

    set_bias(0)
    for c in range(kv_heads):
        attend(0, c)
    for c in range(kv_heads):
        forward(1, c)

    @pl.when(srv >= 2)
    def _():
        doc_copy(2).wait_recv()
        set_bias(2)
        for c in range(kv_heads):

            @pl.when(even)
            def _():
                for turn in range(2):
                    kv_copy(2, turn, c).wait_recv()

            attend(2, c)

    @pl.when(srv >= 1)
    def _():
        doc_copy(1).wait_recv()
        set_bias(1)

    def out_copy(c):
        width = REPEAT * HEAD
        column_of = pl.multiple_of(head * kv_heads * width + c * width, width)
        return remote(
            stage.at[c],
            out_ref.at[:, pl.ds(column_of, width)],
            out_send.at[c],
            out_recv.at[c],
            partner,
        )

    for c in range(kv_heads):

        @pl.when(srv >= 1)
        def _():
            for turn in range(2):
                kv_copy(1, turn, c).wait_recv()
            attend(1, c)

        for g in range(REPEAT):
            h = c * REPEAT + g
            stage[c, :, g * HEAD : (g + 1) * HEAD] = result(h, other)
        out_copy(c).start()
        for g in range(REPEAT):
            h = c * REPEAT + g
            at = pl.multiple_of((head * kv_heads + c) * REPEAT * HEAD + g * HEAD, HEAD)
            out_ref[:, pl.ds(at, HEAD)] = result(h, head)

    pair_tok.wait_send()
    pair_doc.wait_send()
    for by in (1, 2):

        @pl.when(srv + by < n)
        def _(by=by):
            doc_copy(by).wait_send()

    for turn in range(2):
        for c in range(kv_heads):

            @pl.when(sends_two)
            def _():
                kv_copy(2, turn, c).wait_send()

            @pl.when(sends_one)
            def _():
                kv_copy(1, turn, c).wait_send()

            @pl.when(forwards)
            def _():
                kv_forward(turn, c).wait_send()

    for c in range(kv_heads):
        out_copy(c).wait()


def on_device(n, tokens, doc_ids, w_query, w_key, value_weight):
    tok_dev, width = tokens.shape
    kv_heads = w_key.shape[1] // HEAD
    heads = w_query.shape[1] // HEAD
    q_blocks = heads // 2
    bf16, f32 = jnp.bfloat16, jnp.float32
    dma = pltpu.SemaphoreType.DMA
    return pl.pallas_call(
        functools.partial(kernel, n),
        out_shape=jax.ShapeDtypeStruct((tok_dev, 2 * heads * HEAD), bf16),
        in_specs=[pl.BlockSpec(memory_space=pltpu.HBM)] * 5,
        out_specs=pl.BlockSpec(memory_space=pltpu.VMEM),
        scratch_shapes=[
            pltpu.VMEM((2, tok_dev, width), bf16),
            pltpu.VMEM((kv_heads, width, 2 * HEAD), bf16),
            pltpu.VMEM((q_blocks, width, 2 * HEAD), bf16),
            pltpu.VMEM((3, kv_heads, 2, tok_dev, 2 * HEAD), bf16),
            pltpu.VMEM((heads, 2 * tok_dev, HEAD), bf16),
            pltpu.VMEM((heads, 2, HEAD + ONES, tok_dev), f32),
            pltpu.VMEM((heads, 2, 1, tok_dev), f32),
            pltpu.VMEM((3, 2, 2 * tok_dev, tok_dev), f32),
            pltpu.VMEM((6, 1, tok_dev), jnp.int32),
            pltpu.VMEM((kv_heads, tok_dev, REPEAT * HEAD), bf16),
            dma,
            dma((kv_heads, 2)),
            dma((q_blocks,)),
            dma,
            dma((2,)),
            dma((2,)),
            dma((2,)),
            dma((2,)),
            dma((2, 2, kv_heads)),
            dma((2, 2, kv_heads)),
            dma((kv_heads,)),
            dma((kv_heads,)),
        ],
        compiler_params=pltpu.CompilerParams(
            collective_id=0, has_side_effects=True, vmem_limit_bytes=53 * 1024 * 1024
        ),
    )(tokens, doc_ids.reshape(1, tok_dev), w_query, w_key, value_weight)


def solution(mesh):
    in_specs = (
        P(("srv", "head"), None),
        P(("srv", "head")),
        P(None, "head"),
        P(None, "head"),
        P(None, "head"),
    )
    return jax.shard_map(
        functools.partial(on_device, mesh.shape["srv"]),
        mesh=mesh,
        in_specs=in_specs,
        out_specs=P(("srv", "head"), None),
        check_vma=False,
    )
```

```python
import functools
import math

import jax
import jax.numpy as jnp
from jax import lax
from jax.experimental import pallas as pl
from jax.experimental.pallas import tpu as pltpu
from jax.sharding import PartitionSpec as P

HEAD = 128
REPEAT = 4
EXP2_SCALE = math.log2(math.e) / math.sqrt(HEAD)
MASKED = -1e30
ONES = 16
ROW_BLOCKS = 4
MESH = pl.DeviceIdType.MESH


def kernel(
    n,
    tok_hbm,
    doc_hbm,
    wq_hbm,
    wk_hbm,
    wv_hbm,
    out_ref,
    tok,
    wkv,
    wq,
    kv,
    q,
    q_sum,
    acc,
    top,
    bias,
    docs,
    stage,
    tok_sem,
    wkv_sem,
    wq_sem,
    doc_sem,
    pair_send,
    pair_recv,
    doc_send,
    doc_recv,
    kv_send,
    kv_recv,
    out_send,
    out_recv,
):
    srv = lax.axis_index("srv")
    head = lax.axis_index("head")
    other = 1 - head
    tok_dev = tok.shape[1]
    kv_heads = wkv.shape[2] // HEAD
    q_blocks = wq.shape[2] // 256
    even = srv % 2 == 0
    odd = srv % 2 == 1

    def local(src, dst, sem):
        return pltpu.make_async_copy(src, dst, sem)

    own_tok = local(tok_hbm, tok.at[head], tok_sem)
    own_doc = local(doc_hbm, docs.at[head], doc_sem)
    wkv_copies = (
        local(wk_hbm, wkv.at[0], wkv_sem.at[0]),
        local(wv_hbm, wkv.at[1], wkv_sem.at[1]),
    )
    depth = wq.shape[1]
    wq_copies = [
        local(wq_hbm.at[pl.ds(j * depth, depth)], wq.at[j], wq_sem.at[j])
        for j in range(wq.shape[0])
    ]
    own_tok.start()
    own_doc.start()
    for copy in wkv_copies:
        copy.start()

    barrier = pltpu.get_barrier_semaphore()
    pl.semaphore_signal(barrier, inc=1, device_id=(srv, other), device_id_type=MESH)
    count = jnp.int32(1)
    for by in (-2, -1, 1, 2):
        there = (srv + by >= 0) & (srv + by < n)
        count = count + there.astype(jnp.int32)

        @pl.when(there)
        def _(by=by):
            pl.semaphore_signal(barrier, inc=1, device_id=(srv + by, head), device_id_type=MESH)

    pl.semaphore_wait(barrier, count)

    def remote(src, dst, send, recv, device):
        return pltpu.make_async_remote_copy(
            src_ref=src,
            dst_ref=dst,
            send_sem=send,
            recv_sem=recv,
            device_id=device,
            device_id_type=MESH,
        )

    partner = (srv, other)
    pair_tok = remote(tok_hbm, tok.at[head], pair_send.at[0], pair_recv.at[0], partner)
    pair_doc = remote(doc_hbm, docs.at[head], pair_send.at[1], pair_recv.at[1], partner)
    pair_doc.start()
    pair_tok.start()
    for copy in wq_copies:
        copy.start()

    def doc_copy(by):
        return remote(
            docs.at[pl.ds(0, 2)],
            docs.at[pl.ds(2 * by, 2)],
            doc_send.at[by - 1],
            doc_recv.at[by - 1],
            (srv + by, head),
        )

    halves = (head, other)

    def kv_copy(by, turn, c):
        return remote(
            kv.at[0, c, halves[turn]],
            kv.at[by, c, halves[turn]],
            kv_send.at[by - 1, turn, c],
            kv_recv.at[by - 1, turn, c],
            (srv + by, head),
        )

    def kv_forward(turn, c):
        return remote(
            kv.at[2, c, halves[turn]],
            kv.at[1, c, halves[turn]],
            kv_send.at[0, turn, c],
            kv_recv.at[0, turn, c],
            (srv - 1, head),
        )

    sends_one = even & (srv + 1 < n)
    sends_two = srv + 2 < n
    forwards = odd & (srv >= 2)

    def project_kv(turn, first):
        half = halves[turn]
        if first:
            wkv_copies[0].wait()
        keys = jnp.dot(tok[half], wkv[0], preferred_element_type=jnp.float32)
        if first:
            wkv_copies[1].wait()
        values = jnp.dot(tok[half], wkv[1], preferred_element_type=jnp.float32)
        for c in range(kv_heads):
            cols = slice(c * HEAD, (c + 1) * HEAD)
            kv[0, c, half, :, :HEAD] = keys[:, cols].astype(jnp.bfloat16)
            kv[0, c, half, :, HEAD:] = jnp.transpose(values[:, cols]).astype(jnp.bfloat16)

            @pl.when(sends_two)
            def _():
                kv_copy(2, turn, c).start()

            @pl.when(sends_one)
            def _():
                kv_copy(1, turn, c).start()

    def project_q(block):
        rows = tok[:, :, block * depth : (block + 1) * depth].reshape(2 * tok_dev, depth)
        for j in range(q_blocks):
            part = jnp.dot(
                rows, wq[block, :, j * 256 : (j + 1) * 256], preferred_element_type=jnp.float32
            )
            if block:
                part = part + q_sum[j]
            if block + 1 < len(wq_copies):
                q_sum[j] = part
            else:
                q[2 * j] = part[:, :HEAD].astype(jnp.bfloat16)
                q[2 * j + 1] = part[:, HEAD:].astype(jnp.bfloat16)

    def forward(turn, c):
        @pl.when(forwards)
        def _():
            kv_copy(2, turn, c).wait_recv()
            kv_forward(turn, c).start()

    own_tok.wait()
    own_doc.wait()
    project_kv(0, True)
    pair_doc.wait_recv()
    for by in (1, 2):

        @pl.when(srv + by < n)
        def _(by=by):
            doc_copy(by).start()

    pair_tok.wait_recv()
    project_kv(1, False)
    for block in range(len(wq_copies)):
        if block == 2:
            for c in range(kv_heads):
                forward(0, c)
        wq_copies[block].wait()
        project_q(block)

    def column(part):
        ids = docs[part].astype(jnp.float32)
        return jnp.transpose(jnp.broadcast_to(ids, (HEAD, HEAD)))

    def set_bias(block):
        for s in range(2):
            theirs = column(2 * block + s)
            for r in range(2):
                mine = docs[r].astype(jnp.float32)
                allowed = theirs == mine
                if block == 0:
                    keys = lax.broadcasted_iota(jnp.int32, (HEAD, HEAD), 0) + s * HEAD
                    queries = lax.broadcasted_iota(jnp.int32, (HEAD, HEAD), 1) + r * HEAD
                    allowed = allowed & (keys <= queries)
                bias[block, r, s * HEAD : (s + 1) * HEAD, :] = jnp.where(allowed, 0.0, MASKED)

    first_key = {0: (0, 0), 1: (0, 0), 2: (0, tok_dev)}
    last_key = {0: (tok_dev, 2 * tok_dev), 1: (2 * tok_dev,) * 2, 2: (2 * tok_dev,) * 2}

    def attend(block, c):
        keys = kv[block, c].reshape(2 * tok_dev, 2 * HEAD)[:, :HEAD]
        values = jnp.concatenate([kv[block, c, 0, :, HEAD:], kv[block, c, 1, :, HEAD:]], axis=1)
        values = jnp.concatenate([values, jnp.ones((ONES, 2 * tok_dev), jnp.bfloat16)], axis=0)
        for g in range(REPEAT):
            h = c * REPEAT + g
            for r in range(2):
                lo, hi = first_key[block][r], last_key[block][r]
                score = lax.dot_general(
                    keys[lo:hi],
                    q[h, r * tok_dev : (r + 1) * tok_dev],
                    (((1,), (1,)), ((), ())),
                    preferred_element_type=jnp.float32,
                )
                score = score + bias[block, r, lo:hi]
                high = jnp.max(score, axis=0, keepdims=True)
                if block:
                    before = top[h, r]
                    high = jnp.maximum(high, before)
                weight = jnp.exp2((score - high) * EXP2_SCALE).astype(jnp.bfloat16)
                part = jnp.dot(values[:, lo:hi], weight, preferred_element_type=jnp.float32)
                if block:
                    part = part + acc[h, r] * jnp.exp2((before - high) * EXP2_SCALE)
                acc[h, r] = part
                if block != 1:
                    top[h, r] = high

    identity = (
        lax.broadcasted_iota(jnp.int32, (tok_dev, tok_dev), 0)
        == lax.broadcasted_iota(jnp.int32, (tok_dev, tok_dev), 1)
    ).astype(jnp.bfloat16)

    def result(h, half):
        total = acc[h, half, HEAD : HEAD + 1]
        rounded = (acc[h, half, :HEAD] * (1.0 / total)).astype(jnp.bfloat16)
        return lax.dot_general(
            identity, rounded, (((1,), (1,)), ((), ())), preferred_element_type=jnp.float32
        ).astype(jnp.bfloat16)

    set_bias(0)
    for c in range(kv_heads):
        attend(0, c)
    for c in range(kv_heads):
        forward(1, c)

    @pl.when(srv >= 2)
    def _():
        doc_copy(2).wait_recv()
        set_bias(2)
        for c in range(kv_heads):

            @pl.when(even)
            def _():
                for turn in range(2):
                    kv_copy(2, turn, c).wait_recv()

            attend(2, c)

    @pl.when(srv >= 1)
    def _():
        doc_copy(1).wait_recv()
        set_bias(1)

    def out_copy(c):
        width = REPEAT * HEAD
        column_of = pl.multiple_of(head * kv_heads * width + c * width, width)
        return remote(
            stage.at[c],
            out_ref.at[:, pl.ds(column_of, width)],
            out_send.at[c],
            out_recv.at[c],
            partner,
        )

    for c in range(kv_heads):

        @pl.when(srv >= 1)
        def _():
            for turn in range(2):
                kv_copy(1, turn, c).wait_recv()
            attend(1, c)

        for g in range(REPEAT):
            h = c * REPEAT + g
            stage[c, :, g * HEAD : (g + 1) * HEAD] = result(h, other)
        out_copy(c).start()
        for g in range(REPEAT):
            h = c * REPEAT + g
            at = pl.multiple_of((head * kv_heads + c) * REPEAT * HEAD + g * HEAD, HEAD)
            out_ref[:, pl.ds(at, HEAD)] = result(h, head)

    pair_tok.wait_send()
    pair_doc.wait_send()
    for by in (1, 2):

        @pl.when(srv + by < n)
        def _(by=by):
            doc_copy(by).wait_send()

    for turn in range(2):
        for c in range(kv_heads):

            @pl.when(sends_two)
            def _():
                kv_copy(2, turn, c).wait_send()

            @pl.when(sends_one)
            def _():
                kv_copy(1, turn, c).wait_send()

            @pl.when(forwards)
            def _():
                kv_forward(turn, c).wait_send()

    for c in range(kv_heads):
        out_copy(c).wait()


def on_device(n, tokens, doc_ids, w_query, w_key, value_weight):
    tok_dev, width = tokens.shape
    kv_heads = w_key.shape[1] // HEAD
    heads = w_query.shape[1] // HEAD
    q_blocks = heads // 2
    bf16, f32 = jnp.bfloat16, jnp.float32
    dma = pltpu.SemaphoreType.DMA
    return pl.pallas_call(
        functools.partial(kernel, n),
        out_shape=jax.ShapeDtypeStruct((tok_dev, 2 * heads * HEAD), bf16),
        in_specs=[pl.BlockSpec(memory_space=pltpu.HBM)] * 5,
        out_specs=pl.BlockSpec(memory_space=pltpu.VMEM),
        scratch_shapes=[
            pltpu.VMEM((2, tok_dev, width), bf16),
            pltpu.VMEM((2, width, kv_heads * HEAD), bf16),
            pltpu.VMEM((ROW_BLOCKS, width // ROW_BLOCKS, heads * HEAD), bf16),
            pltpu.VMEM((3, kv_heads, 2, tok_dev, 2 * HEAD), bf16),
            pltpu.VMEM((heads, 2 * tok_dev, HEAD), bf16),
            pltpu.VMEM((q_blocks, 2 * tok_dev, 256), f32),
            pltpu.VMEM((heads, 2, HEAD + ONES, tok_dev), f32),
            pltpu.VMEM((heads, 2, 1, tok_dev), f32),
            pltpu.VMEM((3, 2, 2 * tok_dev, tok_dev), f32),
            pltpu.VMEM((6, 1, tok_dev), jnp.int32),
            pltpu.VMEM((kv_heads, tok_dev, REPEAT * HEAD), bf16),
            dma,
            dma((2,)),
            dma((ROW_BLOCKS,)),
            dma,
            dma((2,)),
            dma((2,)),
            dma((2,)),
            dma((2,)),
            dma((2, 2, kv_heads)),
            dma((2, 2, kv_heads)),
            dma((kv_heads,)),
            dma((kv_heads,)),
        ],
        compiler_params=pltpu.CompilerParams(
            collective_id=0, has_side_effects=True, vmem_limit_bytes=53 * 1024 * 1024
        ),
    )(tokens, doc_ids.reshape(1, tok_dev), w_query, w_key, value_weight)


def solution(mesh):
    in_specs = (
        P(("srv", "head"), None),
        P(("srv", "head")),
        P(None, "head"),
        P(None, "head"),
        P(None, "head"),
    )
    return jax.shard_map(
        functools.partial(on_device, mesh.shape["srv"]),
        mesh=mesh,
        in_specs=in_specs,
        out_specs=P(("srv", "head"), None),
        check_vma=False,
    )
```

```python
import functools
import math

import jax
import jax.numpy as jnp
from jax import lax
from jax.experimental import pallas as pl
from jax.experimental.pallas import tpu as pltpu
from jax.sharding import PartitionSpec as P

HEAD = 128
REPEAT = 4
EXP2_SCALE = math.log2(math.e) / math.sqrt(HEAD)
MASKED = -1e30
ONES = 16
ROW_BLOCKS = 4
MESH = pl.DeviceIdType.MESH


def kernel(
    n,
    tok_hbm,
    doc_hbm,
    wq_hbm,
    wk_hbm,
    wv_hbm,
    out_ref,
    tok,
    wkv,
    wq,
    kv,
    q,
    q_sum,
    acc,
    top,
    bias,
    docs,
    stage,
    tok_sem,
    wkv_sem,
    wq_sem,
    doc_sem,
    pair_send,
    pair_recv,
    doc_send,
    doc_recv,
    kv_send,
    kv_recv,
    out_send,
    out_recv,
):
    srv = lax.axis_index("srv")
    head = lax.axis_index("head")
    other = 1 - head
    tok_dev = tok.shape[1]
    kv_heads = wkv.shape[2] // HEAD
    q_blocks = wq.shape[2] // 256
    even = srv % 2 == 0
    odd = srv % 2 == 1

    def local(src, dst, sem):
        return pltpu.make_async_copy(src, dst, sem)

    own_tok = local(tok_hbm, tok.at[head], tok_sem)
    own_doc = local(doc_hbm, docs.at[head], doc_sem)
    wkv_copies = (
        local(wk_hbm, wkv.at[0], wkv_sem.at[0]),
        local(wv_hbm, wkv.at[1], wkv_sem.at[1]),
    )
    depth = wq.shape[1]
    wq_copies = [
        local(wq_hbm.at[pl.ds(j * depth, depth)], wq.at[j], wq_sem.at[j])
        for j in range(wq.shape[0])
    ]
    own_tok.start()
    own_doc.start()
    for copy in wkv_copies:
        copy.start()

    barrier = pltpu.get_barrier_semaphore()
    pl.semaphore_signal(barrier, inc=1, device_id=(srv, other), device_id_type=MESH)
    count = jnp.int32(1)
    for by in (-2, -1, 1, 2):
        there = (srv + by >= 0) & (srv + by < n)
        count = count + there.astype(jnp.int32)

        @pl.when(there)
        def _(by=by):
            pl.semaphore_signal(barrier, inc=1, device_id=(srv + by, head), device_id_type=MESH)

    pl.semaphore_wait(barrier, count)

    def remote(src, dst, send, recv, device):
        return pltpu.make_async_remote_copy(
            src_ref=src,
            dst_ref=dst,
            send_sem=send,
            recv_sem=recv,
            device_id=device,
            device_id_type=MESH,
        )

    partner = (srv, other)
    pair_tok = remote(tok_hbm, tok.at[head], pair_send.at[0], pair_recv.at[0], partner)
    pair_doc = remote(doc_hbm, docs.at[head], pair_send.at[1], pair_recv.at[1], partner)
    pair_doc.start()
    pair_tok.start()
    for copy in wq_copies:
        copy.start()

    def doc_copy(by):
        return remote(
            docs.at[pl.ds(0, 2)],
            docs.at[pl.ds(2 * by, 2)],
            doc_send.at[by - 1],
            doc_recv.at[by - 1],
            (srv + by, head),
        )

    halves = (head, other)

    def kv_copy(by, turn, c):
        return remote(
            kv.at[0, c, halves[turn]],
            kv.at[by, c, halves[turn]],
            kv_send.at[by - 1, turn, c],
            kv_recv.at[by - 1, turn, c],
            (srv + by, head),
        )

    def kv_forward(turn, c):
        return remote(
            kv.at[2, c, halves[turn]],
            kv.at[1, c, halves[turn]],
            kv_send.at[0, turn, c],
            kv_recv.at[0, turn, c],
            (srv - 1, head),
        )

    sends_one = even & (srv + 1 < n)
    sends_two = srv + 2 < n
    forwards = odd & (srv >= 2)

    def project_kv(turn, first):
        half = halves[turn]
        if first:
            wkv_copies[0].wait()
        keys = jnp.dot(tok[half], wkv[0], preferred_element_type=jnp.float32)
        if first:
            wkv_copies[1].wait()
        values = jnp.dot(tok[half], wkv[1], preferred_element_type=jnp.float32)
        for c in range(kv_heads):
            cols = slice(c * HEAD, (c + 1) * HEAD)
            kv[0, c, half, :, :HEAD] = keys[:, cols].astype(jnp.bfloat16)
            kv[0, c, half, :, HEAD:] = jnp.transpose(values[:, cols]).astype(jnp.bfloat16)

            @pl.when(sends_two)
            def _():
                kv_copy(2, turn, c).start()

            @pl.when(sends_one)
            def _():
                kv_copy(1, turn, c).start()

    def project_q(block):
        rows = tok[:, :, block * depth : (block + 1) * depth].reshape(2 * tok_dev, depth)
        for j in range(q_blocks):
            part = jnp.dot(
                rows, wq[block, :, j * 256 : (j + 1) * 256], preferred_element_type=jnp.float32
            )
            if block:
                part = part + q_sum[j]
            if block + 1 < len(wq_copies):
                q_sum[j] = part
            else:
                q[2 * j] = part[:, :HEAD].astype(jnp.bfloat16)
                q[2 * j + 1] = part[:, HEAD:].astype(jnp.bfloat16)

    def forward(turn, c):
        @pl.when(forwards)
        def _():
            kv_copy(2, turn, c).wait_recv()
            kv_forward(turn, c).start()

    own_tok.wait()
    own_doc.wait()
    project_kv(0, True)
    pair_doc.wait_recv()
    for by in (1, 2):

        @pl.when(srv + by < n)
        def _(by=by):
            doc_copy(by).start()

    pair_tok.wait_recv()
    project_kv(1, False)
    for block in range(len(wq_copies)):
        wq_copies[block].wait()
        project_q(block)
    for c in range(kv_heads):
        forward(0, c)

    def column(part):
        ids = docs[part].astype(jnp.float32)
        return jnp.transpose(jnp.broadcast_to(ids, (HEAD, HEAD)))

    def set_bias(block):
        for s in range(2):
            theirs = column(2 * block + s)
            for r in range(2):
                mine = docs[r].astype(jnp.float32)
                allowed = theirs == mine
                if block == 0:
                    keys = lax.broadcasted_iota(jnp.int32, (HEAD, HEAD), 0) + s * HEAD
                    queries = lax.broadcasted_iota(jnp.int32, (HEAD, HEAD), 1) + r * HEAD
                    allowed = allowed & (keys <= queries)
                bias[block, r, s * HEAD : (s + 1) * HEAD, :] = jnp.where(allowed, 0.0, MASKED)

    first_key = {0: (0, 0), 1: (0, 0), 2: (0, tok_dev)}
    last_key = {0: (tok_dev, 2 * tok_dev), 1: (2 * tok_dev,) * 2, 2: (2 * tok_dev,) * 2}

    def attend(block, c):
        keys = kv[block, c].reshape(2 * tok_dev, 2 * HEAD)[:, :HEAD]
        values = jnp.concatenate([kv[block, c, 0, :, HEAD:], kv[block, c, 1, :, HEAD:]], axis=1)
        values = jnp.concatenate([values, jnp.ones((ONES, 2 * tok_dev), jnp.bfloat16)], axis=0)
        for g in range(REPEAT):
            h = c * REPEAT + g
            for r in range(2):
                lo, hi = first_key[block][r], last_key[block][r]
                score = lax.dot_general(
                    keys[lo:hi],
                    q[h, r * tok_dev : (r + 1) * tok_dev],
                    (((1,), (1,)), ((), ())),
                    preferred_element_type=jnp.float32,
                )
                score = score + bias[block, r, lo:hi]
                high = jnp.max(score, axis=0, keepdims=True)
                if block:
                    before = top[h, r]
                    high = jnp.maximum(high, before)
                weight = jnp.exp2((score - high) * EXP2_SCALE).astype(jnp.bfloat16)
                part = jnp.dot(values[:, lo:hi], weight, preferred_element_type=jnp.float32)
                if block:
                    part = part + acc[h, r] * jnp.exp2((before - high) * EXP2_SCALE)
                acc[h, r] = part
                if block != 1:
                    top[h, r] = high

    identity = (
        lax.broadcasted_iota(jnp.int32, (tok_dev, tok_dev), 0)
        == lax.broadcasted_iota(jnp.int32, (tok_dev, tok_dev), 1)
    ).astype(jnp.bfloat16)

    def result(h, half):
        total = acc[h, half, HEAD : HEAD + 1]
        rounded = (acc[h, half, :HEAD] * (1.0 / total)).astype(jnp.bfloat16)
        return lax.dot_general(
            identity, rounded, (((1,), (1,)), ((), ())), preferred_element_type=jnp.float32
        ).astype(jnp.bfloat16)

    set_bias(0)
    for c in range(kv_heads):
        attend(0, c)
    for c in range(kv_heads):
        forward(1, c)

    @pl.when(srv >= 2)
    def _():
        doc_copy(2).wait_recv()
        set_bias(2)
        for c in range(kv_heads):

            @pl.when(even)
            def _():
                for turn in range(2):
                    kv_copy(2, turn, c).wait_recv()

            attend(2, c)

    @pl.when(srv >= 1)
    def _():
        doc_copy(1).wait_recv()
        set_bias(1)

    def out_copy(c):
        width = REPEAT * HEAD
        column_of = pl.multiple_of(head * kv_heads * width + c * width, width)
        return remote(
            stage.at[c],
            out_ref.at[:, pl.ds(column_of, width)],
            out_send.at[c],
            out_recv.at[c],
            partner,
        )

    for c in range(kv_heads):

        @pl.when(srv >= 1)
        def _():
            for turn in range(2):
                kv_copy(1, turn, c).wait_recv()
            attend(1, c)

        for g in range(REPEAT):
            h = c * REPEAT + g
            stage[c, :, g * HEAD : (g + 1) * HEAD] = result(h, other)
        out_copy(c).start()
        for g in range(REPEAT):
            h = c * REPEAT + g
            at = pl.multiple_of((head * kv_heads + c) * REPEAT * HEAD + g * HEAD, HEAD)
            out_ref[:, pl.ds(at, HEAD)] = result(h, head)

    pair_tok.wait_send()
    pair_doc.wait_send()
    for by in (1, 2):

        @pl.when(srv + by < n)
        def _(by=by):
            doc_copy(by).wait_send()

    for turn in range(2):
        for c in range(kv_heads):

            @pl.when(sends_two)
            def _():
                kv_copy(2, turn, c).wait_send()

            @pl.when(sends_one)
            def _():
                kv_copy(1, turn, c).wait_send()

            @pl.when(forwards)
            def _():
                kv_forward(turn, c).wait_send()

    for c in range(kv_heads):
        out_copy(c).wait()


def on_device(n, tokens, doc_ids, w_query, w_key, value_weight):
    tok_dev, width = tokens.shape
    kv_heads = w_key.shape[1] // HEAD
    heads = w_query.shape[1] // HEAD
    q_blocks = heads // 2
    bf16, f32 = jnp.bfloat16, jnp.float32
    dma = pltpu.SemaphoreType.DMA
    return pl.pallas_call(
        functools.partial(kernel, n),
        out_shape=jax.ShapeDtypeStruct((tok_dev, 2 * heads * HEAD), bf16),
        in_specs=[pl.BlockSpec(memory_space=pltpu.HBM)] * 5,
        out_specs=pl.BlockSpec(memory_space=pltpu.VMEM),
        scratch_shapes=[
            pltpu.VMEM((2, tok_dev, width), bf16),
            pltpu.VMEM((2, width, kv_heads * HEAD), bf16),
            pltpu.VMEM((ROW_BLOCKS, width // ROW_BLOCKS, heads * HEAD), bf16),
            pltpu.VMEM((3, kv_heads, 2, tok_dev, 2 * HEAD), bf16),
            pltpu.VMEM((heads, 2 * tok_dev, HEAD), bf16),
            pltpu.VMEM((q_blocks, 2 * tok_dev, 256), f32),
            pltpu.VMEM((heads, 2, HEAD + ONES, tok_dev), f32),
            pltpu.VMEM((heads, 2, 1, tok_dev), f32),
            pltpu.VMEM((3, 2, 2 * tok_dev, tok_dev), f32),
            pltpu.VMEM((6, 1, tok_dev), jnp.int32),
            pltpu.VMEM((kv_heads, tok_dev, REPEAT * HEAD), bf16),
            dma,
            dma((2,)),
            dma((ROW_BLOCKS,)),
            dma,
            dma((2,)),
            dma((2,)),
            dma((2,)),
            dma((2,)),
            dma((2, 2, kv_heads)),
            dma((2, 2, kv_heads)),
            dma((kv_heads,)),
            dma((kv_heads,)),
        ],
        compiler_params=pltpu.CompilerParams(
            collective_id=0, has_side_effects=True, vmem_limit_bytes=53 * 1024 * 1024
        ),
    )(tokens, doc_ids.reshape(1, tok_dev), w_query, w_key, value_weight)


def solution(mesh):
    in_specs = (
        P(("srv", "head"), None),
        P(("srv", "head")),
        P(None, "head"),
        P(None, "head"),
        P(None, "head"),
    )
    return jax.shard_map(
        functools.partial(on_device, mesh.shape["srv"]),
        mesh=mesh,
        in_specs=in_specs,
        out_specs=P(("srv", "head"), None),
        check_vma=False,
    )
```

```python
import functools
import math

import jax
import jax.numpy as jnp
from jax import lax
from jax.experimental import pallas as pl
from jax.experimental.pallas import tpu as pltpu
from jax.sharding import PartitionSpec as P

HEAD = 128
REPEAT = 4
EXP2_SCALE = math.log2(math.e) / math.sqrt(HEAD)
MASKED = -1e30
ONES = 16
ROW_BLOCKS = 4
TOK_PIECES = 4
MESH = pl.DeviceIdType.MESH


def kernel(
    n,
    tok_hbm,
    doc_hbm,
    wq_hbm,
    wk_hbm,
    wv_hbm,
    out_ref,
    tok,
    wkv,
    wq,
    kv,
    q,
    q_sum,
    acc,
    top,
    bias,
    docs,
    stage,
    tok_sem,
    wkv_sem,
    wq_sem,
    doc_sem,
    pair_send,
    pair_recv,
    doc_send,
    doc_recv,
    kv_send,
    kv_recv,
    out_send,
    out_recv,
):
    srv = lax.axis_index("srv")
    head = lax.axis_index("head")
    other = 1 - head
    tok_dev = tok.shape[1]
    kv_heads = wkv.shape[2] // HEAD
    q_blocks = wq.shape[2] // 256
    even = srv % 2 == 0
    odd = srv % 2 == 1

    def local(src, dst, sem):
        return pltpu.make_async_copy(src, dst, sem)

    own_tok = local(tok_hbm, tok.at[head], tok_sem)
    own_doc = local(doc_hbm, docs.at[head], doc_sem)
    wkv_copies = (
        local(wk_hbm, wkv.at[0], wkv_sem.at[0]),
        local(wv_hbm, wkv.at[1], wkv_sem.at[1]),
    )
    depth = wq.shape[1]
    wq_copies = [
        local(wq_hbm.at[pl.ds(j * depth, depth)], wq.at[j], wq_sem.at[j])
        for j in range(wq.shape[0])
    ]
    own_tok.start()
    own_doc.start()
    for copy in wkv_copies:
        copy.start()

    barrier = pltpu.get_barrier_semaphore()
    pl.semaphore_signal(barrier, inc=1, device_id=(srv, other), device_id_type=MESH)
    count = jnp.int32(1)
    for by in (-2, -1, 1, 2):
        there = (srv + by >= 0) & (srv + by < n)
        count = count + there.astype(jnp.int32)

        @pl.when(there)
        def _(by=by):
            pl.semaphore_signal(barrier, inc=1, device_id=(srv + by, head), device_id_type=MESH)

    pl.semaphore_wait(barrier, count)

    def remote(src, dst, send, recv, device):
        return pltpu.make_async_remote_copy(
            src_ref=src,
            dst_ref=dst,
            send_sem=send,
            recv_sem=recv,
            device_id=device,
            device_id_type=MESH,
        )

    partner = (srv, other)
    piece = tok_dev // TOK_PIECES
    pair_tok = []
    for p in range(TOK_PIECES):
        rows = tok.at[head, pl.ds(p * piece, piece)]
        pair_tok.append(remote(rows, rows, pair_send.at[1 + p], pair_recv.at[1 + p], partner))
    pair_doc = remote(doc_hbm, docs.at[head], pair_send.at[0], pair_recv.at[0], partner)
    pair_doc.start()
    own_tok.wait()
    for copy in pair_tok:
        copy.start()
    for copy in wq_copies:
        copy.start()

    def doc_copy(by):
        return remote(
            docs.at[pl.ds(0, 2)],
            docs.at[pl.ds(2 * by, 2)],
            doc_send.at[by - 1],
            doc_recv.at[by - 1],
            (srv + by, head),
        )

    halves = (head, other)

    def kv_copy(by, turn, c):
        return remote(
            kv.at[0, c, halves[turn]],
            kv.at[by, c, halves[turn]],
            kv_send.at[by - 1, turn, c],
            kv_recv.at[by - 1, turn, c],
            (srv + by, head),
        )

    def kv_forward(turn, c):
        return remote(
            kv.at[2, c, halves[turn]],
            kv.at[1, c, halves[turn]],
            kv_send.at[0, turn, c],
            kv_recv.at[0, turn, c],
            (srv - 1, head),
        )

    sends_one = even & (srv + 1 < n)
    sends_two = srv + 2 < n
    forwards = odd & (srv >= 2)

    def project_kv(turn, first):
        half = halves[turn]
        if first:
            wkv_copies[0].wait()
        keys = jnp.dot(tok[half], wkv[0], preferred_element_type=jnp.float32)
        if first:
            wkv_copies[1].wait()
        values = jnp.dot(tok[half], wkv[1], preferred_element_type=jnp.float32)
        for c in range(kv_heads):
            cols = slice(c * HEAD, (c + 1) * HEAD)
            kv[0, c, half, :, :HEAD] = keys[:, cols].astype(jnp.bfloat16)
            kv[0, c, half, :, HEAD:] = jnp.transpose(values[:, cols]).astype(jnp.bfloat16)

            @pl.when(sends_two)
            def _():
                kv_copy(2, turn, c).start()

            @pl.when(sends_one)
            def _():
                kv_copy(1, turn, c).start()

    def project_q(block):
        rows = tok[:, :, block * depth : (block + 1) * depth].reshape(2 * tok_dev, depth)
        for j in range(q_blocks):
            part = jnp.dot(
                rows, wq[block, :, j * 256 : (j + 1) * 256], preferred_element_type=jnp.float32
            )
            if block:
                part = part + q_sum[j]
            if block + 1 < len(wq_copies):
                q_sum[j] = part
            else:
                q[2 * j] = part[:, :HEAD].astype(jnp.bfloat16)
                q[2 * j + 1] = part[:, HEAD:].astype(jnp.bfloat16)

    def forward(turn, c):
        @pl.when(forwards)
        def _():
            kv_copy(2, turn, c).wait_recv()
            kv_forward(turn, c).start()

    own_doc.wait()
    project_kv(0, True)
    pair_doc.wait_recv()
    for by in (1, 2):

        @pl.when(srv + by < n)
        def _(by=by):
            doc_copy(by).start()

    for copy in pair_tok:
        copy.wait_recv()
    project_kv(1, False)
    for block in range(len(wq_copies)):
        wq_copies[block].wait()
        project_q(block)
    for c in range(kv_heads):
        forward(0, c)

    def column(part):
        ids = docs[part].astype(jnp.float32)
        return jnp.transpose(jnp.broadcast_to(ids, (HEAD, HEAD)))

    def set_bias(block):
        for s in range(2):
            theirs = column(2 * block + s)
            for r in range(2):
                mine = docs[r].astype(jnp.float32)
                allowed = theirs == mine
                if block == 0:
                    keys = lax.broadcasted_iota(jnp.int32, (HEAD, HEAD), 0) + s * HEAD
                    queries = lax.broadcasted_iota(jnp.int32, (HEAD, HEAD), 1) + r * HEAD
                    allowed = allowed & (keys <= queries)
                bias[block, r, s * HEAD : (s + 1) * HEAD, :] = jnp.where(allowed, 0.0, MASKED)

    first_key = {0: (0, 0), 1: (0, 0), 2: (0, tok_dev)}
    last_key = {0: (tok_dev, 2 * tok_dev), 1: (2 * tok_dev,) * 2, 2: (2 * tok_dev,) * 2}

    def attend(block, c):
        keys = kv[block, c].reshape(2 * tok_dev, 2 * HEAD)[:, :HEAD]
        values = jnp.concatenate([kv[block, c, 0, :, HEAD:], kv[block, c, 1, :, HEAD:]], axis=1)
        values = jnp.concatenate([values, jnp.ones((ONES, 2 * tok_dev), jnp.bfloat16)], axis=0)
        for g in range(REPEAT):
            h = c * REPEAT + g
            for r in range(2):
                lo, hi = first_key[block][r], last_key[block][r]
                score = lax.dot_general(
                    keys[lo:hi],
                    q[h, r * tok_dev : (r + 1) * tok_dev],
                    (((1,), (1,)), ((), ())),
                    preferred_element_type=jnp.float32,
                )
                score = score + bias[block, r, lo:hi]
                high = jnp.max(score, axis=0, keepdims=True)
                if block:
                    before = top[h, r]
                    high = jnp.maximum(high, before)
                weight = jnp.exp2((score - high) * EXP2_SCALE).astype(jnp.bfloat16)
                part = jnp.dot(values[:, lo:hi], weight, preferred_element_type=jnp.float32)
                if block:
                    part = part + acc[h, r] * jnp.exp2((before - high) * EXP2_SCALE)
                acc[h, r] = part
                if block != 1:
                    top[h, r] = high

    identity = (
        lax.broadcasted_iota(jnp.int32, (tok_dev, tok_dev), 0)
        == lax.broadcasted_iota(jnp.int32, (tok_dev, tok_dev), 1)
    ).astype(jnp.bfloat16)

    def result(h, half):
        total = acc[h, half, HEAD : HEAD + 1]
        rounded = (acc[h, half, :HEAD] * (1.0 / total)).astype(jnp.bfloat16)
        return lax.dot_general(
            identity, rounded, (((1,), (1,)), ((), ())), preferred_element_type=jnp.float32
        ).astype(jnp.bfloat16)

    set_bias(0)
    for c in range(kv_heads):
        attend(0, c)
    for c in range(kv_heads):
        forward(1, c)

    @pl.when(srv >= 2)
    def _():
        doc_copy(2).wait_recv()
        set_bias(2)
        for c in range(kv_heads):

            @pl.when(even)
            def _():
                for turn in range(2):
                    kv_copy(2, turn, c).wait_recv()

            attend(2, c)

    @pl.when(srv >= 1)
    def _():
        doc_copy(1).wait_recv()
        set_bias(1)

    def out_copy(c):
        width = REPEAT * HEAD
        column_of = pl.multiple_of(head * kv_heads * width + c * width, width)
        return remote(
            stage.at[c],
            out_ref.at[:, pl.ds(column_of, width)],
            out_send.at[c],
            out_recv.at[c],
            partner,
        )

    for c in range(kv_heads):

        @pl.when(srv >= 1)
        def _():
            for turn in range(2):
                kv_copy(1, turn, c).wait_recv()
            attend(1, c)

        for g in range(REPEAT):
            h = c * REPEAT + g
            stage[c, :, g * HEAD : (g + 1) * HEAD] = result(h, other)
        out_copy(c).start()
        for g in range(REPEAT):
            h = c * REPEAT + g
            at = pl.multiple_of((head * kv_heads + c) * REPEAT * HEAD + g * HEAD, HEAD)
            out_ref[:, pl.ds(at, HEAD)] = result(h, head)

    for copy in pair_tok:
        copy.wait_send()
    pair_doc.wait_send()
    for by in (1, 2):

        @pl.when(srv + by < n)
        def _(by=by):
            doc_copy(by).wait_send()

    for turn in range(2):
        for c in range(kv_heads):

            @pl.when(sends_two)
            def _():
                kv_copy(2, turn, c).wait_send()

            @pl.when(sends_one)
            def _():
                kv_copy(1, turn, c).wait_send()

            @pl.when(forwards)
            def _():
                kv_forward(turn, c).wait_send()

    for c in range(kv_heads):
        out_copy(c).wait()


def on_device(n, tokens, doc_ids, w_query, w_key, value_weight):
    tok_dev, width = tokens.shape
    kv_heads = w_key.shape[1] // HEAD
    heads = w_query.shape[1] // HEAD
    q_blocks = heads // 2
    bf16, f32 = jnp.bfloat16, jnp.float32
    dma = pltpu.SemaphoreType.DMA
    return pl.pallas_call(
        functools.partial(kernel, n),
        out_shape=jax.ShapeDtypeStruct((tok_dev, 2 * heads * HEAD), bf16),
        in_specs=[pl.BlockSpec(memory_space=pltpu.HBM)] * 5,
        out_specs=pl.BlockSpec(memory_space=pltpu.VMEM),
        scratch_shapes=[
            pltpu.VMEM((2, tok_dev, width), bf16),
            pltpu.VMEM((2, width, kv_heads * HEAD), bf16),
            pltpu.VMEM((ROW_BLOCKS, width // ROW_BLOCKS, heads * HEAD), bf16),
            pltpu.VMEM((3, kv_heads, 2, tok_dev, 2 * HEAD), bf16),
            pltpu.VMEM((heads, 2 * tok_dev, HEAD), bf16),
            pltpu.VMEM((q_blocks, 2 * tok_dev, 256), f32),
            pltpu.VMEM((heads, 2, HEAD + ONES, tok_dev), f32),
            pltpu.VMEM((heads, 2, 1, tok_dev), f32),
            pltpu.VMEM((3, 2, 2 * tok_dev, tok_dev), f32),
            pltpu.VMEM((6, 1, tok_dev), jnp.int32),
            pltpu.VMEM((kv_heads, tok_dev, REPEAT * HEAD), bf16),
            dma,
            dma((2,)),
            dma((ROW_BLOCKS,)),
            dma,
            dma((1 + TOK_PIECES,)),
            dma((1 + TOK_PIECES,)),
            dma((2,)),
            dma((2,)),
            dma((2, 2, kv_heads)),
            dma((2, 2, kv_heads)),
            dma((kv_heads,)),
            dma((kv_heads,)),
        ],
        compiler_params=pltpu.CompilerParams(
            collective_id=0, has_side_effects=True, vmem_limit_bytes=53 * 1024 * 1024
        ),
    )(tokens, doc_ids.reshape(1, tok_dev), w_query, w_key, value_weight)


def solution(mesh):
    in_specs = (
        P(("srv", "head"), None),
        P(("srv", "head")),
        P(None, "head"),
        P(None, "head"),
        P(None, "head"),
    )
    return jax.shard_map(
        functools.partial(on_device, mesh.shape["srv"]),
        mesh=mesh,
        in_specs=in_specs,
        out_specs=P(("srv", "head"), None),
        check_vma=False,
    )
```

```python
import functools
import math

import jax
import jax.numpy as jnp
from jax import lax
from jax.experimental import pallas as pl
from jax.experimental.pallas import tpu as pltpu
from jax.sharding import PartitionSpec as P

HEAD = 128
REPEAT = 4
EXP2_SCALE = math.log2(math.e) / math.sqrt(HEAD)
MASKED = -1e30
ONES = 16
ROW_BLOCKS = 4
TOK_PIECES = 4
MESH = pl.DeviceIdType.MESH


def kernel(
    n,
    tok_hbm,
    doc_hbm,
    wq_hbm,
    wk_hbm,
    wv_hbm,
    out_ref,
    tok,
    wkv,
    wq,
    kv,
    q,
    q_sum,
    acc,
    top,
    bias,
    docs,
    stage,
    tok_sem,
    wkv_sem,
    wq_sem,
    doc_sem,
    pair_send,
    pair_recv,
    doc_send,
    doc_recv,
    kv_send,
    kv_recv,
    out_send,
    out_recv,
):
    srv = lax.axis_index("srv")
    head = lax.axis_index("head")
    other = 1 - head
    tok_dev = tok.shape[1]
    kv_heads = wkv.shape[2] // HEAD
    q_blocks = wq.shape[2] // 256
    even = srv % 2 == 0
    odd = srv % 2 == 1

    def local(src, dst, sem):
        return pltpu.make_async_copy(src, dst, sem)

    own_tok = local(tok_hbm, tok.at[head], tok_sem)
    own_doc = local(doc_hbm, docs.at[head], doc_sem)
    wkv_copies = (
        local(wk_hbm, wkv.at[0], wkv_sem.at[0]),
        local(wv_hbm, wkv.at[1], wkv_sem.at[1]),
    )
    depth = wq.shape[1]
    wq_copies = [
        local(wq_hbm.at[pl.ds(j * depth, depth)], wq.at[j], wq_sem.at[j])
        for j in range(wq.shape[0])
    ]
    own_tok.start()
    own_doc.start()
    for copy in wkv_copies:
        copy.start()

    barrier = pltpu.get_barrier_semaphore()
    pl.semaphore_signal(barrier, inc=1, device_id=(srv, other), device_id_type=MESH)
    count = jnp.int32(1)
    for by in (-2, -1, 1, 2):
        there = (srv + by >= 0) & (srv + by < n)
        count = count + there.astype(jnp.int32)

        @pl.when(there)
        def _(by=by):
            pl.semaphore_signal(barrier, inc=1, device_id=(srv + by, head), device_id_type=MESH)

    pl.semaphore_wait(barrier, count)

    def remote(src, dst, send, recv, device):
        return pltpu.make_async_remote_copy(
            src_ref=src,
            dst_ref=dst,
            send_sem=send,
            recv_sem=recv,
            device_id=device,
            device_id_type=MESH,
        )

    partner = (srv, other)
    piece = tok_dev // TOK_PIECES
    pair_tok = []
    for p in range(TOK_PIECES):
        rows = tok.at[head, pl.ds(p * piece, piece)]
        pair_tok.append(remote(rows, rows, pair_send.at[1 + p], pair_recv.at[1 + p], partner))
    pair_doc = remote(doc_hbm, docs.at[head], pair_send.at[0], pair_recv.at[0], partner)
    pair_doc.start()
    own_tok.wait()
    for copy in pair_tok:
        copy.start()
    for copy in wq_copies:
        copy.start()

    def doc_copy(by):
        return remote(
            docs.at[pl.ds(0, 2)],
            docs.at[pl.ds(2 * by, 2)],
            doc_send.at[by - 1],
            doc_recv.at[by - 1],
            (srv + by, head),
        )

    halves = (head, other)

    def kv_copy(by, turn, c):
        return remote(
            kv.at[0, c, halves[turn]],
            kv.at[by, c, halves[turn]],
            kv_send.at[by - 1, turn, c],
            kv_recv.at[by - 1, turn, c],
            (srv + by, head),
        )

    def kv_forward(turn, c):
        return remote(
            kv.at[2, c, halves[turn]],
            kv.at[1, c, halves[turn]],
            kv_send.at[0, turn, c],
            kv_recv.at[0, turn, c],
            (srv - 1, head),
        )

    sends_one = even & (srv + 1 < n)
    sends_two = srv + 2 < n
    forwards = odd & (srv >= 2)

    def relayed(turn, c):
        return (turn, c) != (1, kv_heads - 1)

    def sends_next(turn, c):
        return sends_one if relayed(turn, c) else srv + 1 < n

    def project_kv(turn, first):
        half = halves[turn]
        if first:
            wkv_copies[0].wait()
        keys = jnp.dot(tok[half], wkv[0], preferred_element_type=jnp.float32)
        if first:
            wkv_copies[1].wait()
        values = jnp.dot(tok[half], wkv[1], preferred_element_type=jnp.float32)
        for c in range(kv_heads):
            cols = slice(c * HEAD, (c + 1) * HEAD)
            kv[0, c, half, :, :HEAD] = keys[:, cols].astype(jnp.bfloat16)
            kv[0, c, half, :, HEAD:] = jnp.transpose(values[:, cols]).astype(jnp.bfloat16)

            @pl.when(sends_two)
            def _():
                kv_copy(2, turn, c).start()

            @pl.when(sends_next(turn, c))
            def _():
                kv_copy(1, turn, c).start()

    def project_q(block):
        rows = tok[:, :, block * depth : (block + 1) * depth].reshape(2 * tok_dev, depth)
        for j in range(q_blocks):
            part = jnp.dot(
                rows, wq[block, :, j * 256 : (j + 1) * 256], preferred_element_type=jnp.float32
            )
            if block:
                part = part + q_sum[j]
            if block + 1 < len(wq_copies):
                q_sum[j] = part
            else:
                q[2 * j] = part[:, :HEAD].astype(jnp.bfloat16)
                q[2 * j + 1] = part[:, HEAD:].astype(jnp.bfloat16)

    def forward(turn, c):
        if not relayed(turn, c):
            return

        @pl.when(forwards)
        def _():
            kv_copy(2, turn, c).wait_recv()
            kv_forward(turn, c).start()

    own_doc.wait()
    project_kv(0, True)
    pair_doc.wait_recv()
    for by in (1, 2):

        @pl.when(srv + by < n)
        def _(by=by):
            doc_copy(by).start()

    for copy in pair_tok:
        copy.wait_recv()
    project_kv(1, False)
    for block in range(len(wq_copies)):
        wq_copies[block].wait()
        project_q(block)
    for c in range(kv_heads):
        forward(0, c)

    def column(part):
        ids = docs[part].astype(jnp.float32)
        return jnp.transpose(jnp.broadcast_to(ids, (HEAD, HEAD)))

    def set_bias(block):
        for s in range(2):
            theirs = column(2 * block + s)
            for r in range(2):
                mine = docs[r].astype(jnp.float32)
                allowed = theirs == mine
                if block == 0:
                    keys = lax.broadcasted_iota(jnp.int32, (HEAD, HEAD), 0) + s * HEAD
                    queries = lax.broadcasted_iota(jnp.int32, (HEAD, HEAD), 1) + r * HEAD
                    allowed = allowed & (keys <= queries)
                bias[block, r, s * HEAD : (s + 1) * HEAD, :] = jnp.where(allowed, 0.0, MASKED)

    first_key = {0: (0, 0), 1: (0, 0), 2: (0, tok_dev)}
    last_key = {0: (tok_dev, 2 * tok_dev), 1: (2 * tok_dev,) * 2, 2: (2 * tok_dev,) * 2}

    def attend(block, c):
        keys = kv[block, c].reshape(2 * tok_dev, 2 * HEAD)[:, :HEAD]
        values = jnp.concatenate([kv[block, c, 0, :, HEAD:], kv[block, c, 1, :, HEAD:]], axis=1)
        values = jnp.concatenate([values, jnp.ones((ONES, 2 * tok_dev), jnp.bfloat16)], axis=0)
        for g in range(REPEAT):
            h = c * REPEAT + g
            for r in range(2):
                lo, hi = first_key[block][r], last_key[block][r]
                score = lax.dot_general(
                    keys[lo:hi],
                    q[h, r * tok_dev : (r + 1) * tok_dev],
                    (((1,), (1,)), ((), ())),
                    preferred_element_type=jnp.float32,
                )
                score = score + bias[block, r, lo:hi]
                high = jnp.max(score, axis=0, keepdims=True)
                if block:
                    before = top[h, r]
                    high = jnp.maximum(high, before)
                weight = jnp.exp2((score - high) * EXP2_SCALE).astype(jnp.bfloat16)
                part = jnp.dot(values[:, lo:hi], weight, preferred_element_type=jnp.float32)
                if block:
                    part = part + acc[h, r] * jnp.exp2((before - high) * EXP2_SCALE)
                acc[h, r] = part
                if block != 1:
                    top[h, r] = high

    identity = (
        lax.broadcasted_iota(jnp.int32, (tok_dev, tok_dev), 0)
        == lax.broadcasted_iota(jnp.int32, (tok_dev, tok_dev), 1)
    ).astype(jnp.bfloat16)

    def result(h, half):
        total = acc[h, half, HEAD : HEAD + 1]
        rounded = (acc[h, half, :HEAD] * (1.0 / total)).astype(jnp.bfloat16)
        return lax.dot_general(
            identity, rounded, (((1,), (1,)), ((), ())), preferred_element_type=jnp.float32
        ).astype(jnp.bfloat16)

    set_bias(0)
    for c in range(kv_heads):
        attend(0, c)
    for c in range(kv_heads):
        forward(1, c)

    @pl.when(srv >= 2)
    def _():
        doc_copy(2).wait_recv()
        set_bias(2)
        for c in range(kv_heads):

            for turn in range(2):

                @pl.when(even if relayed(turn, c) else srv >= 2)
                def _():
                    kv_copy(2, turn, c).wait_recv()

            attend(2, c)

    @pl.when(srv >= 1)
    def _():
        doc_copy(1).wait_recv()
        set_bias(1)

    def out_copy(c):
        width = REPEAT * HEAD
        column_of = pl.multiple_of(head * kv_heads * width + c * width, width)
        return remote(
            stage.at[c],
            out_ref.at[:, pl.ds(column_of, width)],
            out_send.at[c],
            out_recv.at[c],
            partner,
        )

    for c in range(kv_heads):

        @pl.when(srv >= 1)
        def _():
            for turn in range(2):
                kv_copy(1, turn, c).wait_recv()
            attend(1, c)

        for g in range(REPEAT):
            h = c * REPEAT + g
            stage[c, :, g * HEAD : (g + 1) * HEAD] = result(h, other)
        out_copy(c).start()
        for g in range(REPEAT):
            h = c * REPEAT + g
            at = pl.multiple_of((head * kv_heads + c) * REPEAT * HEAD + g * HEAD, HEAD)
            out_ref[:, pl.ds(at, HEAD)] = result(h, head)

    for copy in pair_tok:
        copy.wait_send()
    pair_doc.wait_send()
    for by in (1, 2):

        @pl.when(srv + by < n)
        def _(by=by):
            doc_copy(by).wait_send()

    for turn in range(2):
        for c in range(kv_heads):

            @pl.when(sends_two)
            def _():
                kv_copy(2, turn, c).wait_send()

            @pl.when(sends_next(turn, c))
            def _():
                kv_copy(1, turn, c).wait_send()

            if relayed(turn, c):

                @pl.when(forwards)
                def _():
                    kv_forward(turn, c).wait_send()

    for c in range(kv_heads):
        out_copy(c).wait()


def on_device(n, tokens, doc_ids, w_query, w_key, value_weight):
    tok_dev, width = tokens.shape
    kv_heads = w_key.shape[1] // HEAD
    heads = w_query.shape[1] // HEAD
    q_blocks = heads // 2
    bf16, f32 = jnp.bfloat16, jnp.float32
    dma = pltpu.SemaphoreType.DMA
    return pl.pallas_call(
        functools.partial(kernel, n),
        out_shape=jax.ShapeDtypeStruct((tok_dev, 2 * heads * HEAD), bf16),
        in_specs=[pl.BlockSpec(memory_space=pltpu.HBM)] * 5,
        out_specs=pl.BlockSpec(memory_space=pltpu.VMEM),
        scratch_shapes=[
            pltpu.VMEM((2, tok_dev, width), bf16),
            pltpu.VMEM((2, width, kv_heads * HEAD), bf16),
            pltpu.VMEM((ROW_BLOCKS, width // ROW_BLOCKS, heads * HEAD), bf16),
            pltpu.VMEM((3, kv_heads, 2, tok_dev, 2 * HEAD), bf16),
            pltpu.VMEM((heads, 2 * tok_dev, HEAD), bf16),
            pltpu.VMEM((q_blocks, 2 * tok_dev, 256), f32),
            pltpu.VMEM((heads, 2, HEAD + ONES, tok_dev), f32),
            pltpu.VMEM((heads, 2, 1, tok_dev), f32),
            pltpu.VMEM((3, 2, 2 * tok_dev, tok_dev), f32),
            pltpu.VMEM((6, 1, tok_dev), jnp.int32),
            pltpu.VMEM((kv_heads, tok_dev, REPEAT * HEAD), bf16),
            dma,
            dma((2,)),
            dma((ROW_BLOCKS,)),
            dma,
            dma((1 + TOK_PIECES,)),
            dma((1 + TOK_PIECES,)),
            dma((2,)),
            dma((2,)),
            dma((2, 2, kv_heads)),
            dma((2, 2, kv_heads)),
            dma((kv_heads,)),
            dma((kv_heads,)),
        ],
        compiler_params=pltpu.CompilerParams(
            collective_id=0, has_side_effects=True, vmem_limit_bytes=53 * 1024 * 1024
        ),
    )(tokens, doc_ids.reshape(1, tok_dev), w_query, w_key, value_weight)


def solution(mesh):
    in_specs = (
        P(("srv", "head"), None),
        P(("srv", "head")),
        P(None, "head"),
        P(None, "head"),
        P(None, "head"),
    )
    return jax.shard_map(
        functools.partial(on_device, mesh.shape["srv"]),
        mesh=mesh,
        in_specs=in_specs,
        out_specs=P(("srv", "head"), None),
        check_vma=False,
    )
```

```python
import functools
import math

import jax
import jax.numpy as jnp
from jax import lax
from jax.experimental import pallas as pl
from jax.experimental.pallas import tpu as pltpu
from jax.sharding import PartitionSpec as P

HEAD = 128
REPEAT = 4
EXP2_SCALE = math.log2(math.e) / math.sqrt(HEAD)
MASKED = -1e30
ONES = 16
ROW_BLOCKS = 4
TOK_PIECES = 4
MESH = pl.DeviceIdType.MESH


def kernel(
    n,
    tok_hbm,
    doc_hbm,
    wq_hbm,
    wk_hbm,
    wv_hbm,
    out_ref,
    tok,
    wkv,
    wq,
    kv,
    q,
    q_sum,
    acc,
    top,
    bias,
    docs,
    stage,
    tok_sem,
    wkv_sem,
    wq_sem,
    doc_sem,
    pair_send,
    pair_recv,
    doc_send,
    doc_recv,
    kv_send,
    kv_recv,
    out_send,
    out_recv,
):
    srv = lax.axis_index("srv")
    head = lax.axis_index("head")
    other = 1 - head
    tok_dev = tok.shape[1]
    kv_heads = wkv.shape[2] // HEAD
    q_blocks = wq.shape[2] // 256
    even = srv % 2 == 0
    odd = srv % 2 == 1

    def local(src, dst, sem):
        return pltpu.make_async_copy(src, dst, sem)

    own_tok = local(tok_hbm, tok.at[head], tok_sem)
    own_doc = local(doc_hbm, docs.at[head], doc_sem)
    wkv_copies = (
        local(wk_hbm, wkv.at[0], wkv_sem.at[0]),
        local(wv_hbm, wkv.at[1], wkv_sem.at[1]),
    )
    depth = wq.shape[1]
    wq_copies = [
        local(wq_hbm.at[pl.ds(j * depth, depth)], wq.at[j], wq_sem.at[j])
        for j in range(wq.shape[0])
    ]
    own_tok.start()
    own_doc.start()
    for copy in wkv_copies:
        copy.start()

    barrier = pltpu.get_barrier_semaphore()
    pl.semaphore_signal(barrier, inc=1, device_id=(srv, other), device_id_type=MESH)
    count = jnp.int32(1)
    for by in (-2, -1, 1, 2):
        there = (srv + by >= 0) & (srv + by < n)
        count = count + there.astype(jnp.int32)

        @pl.when(there)
        def _(by=by):
            pl.semaphore_signal(barrier, inc=1, device_id=(srv + by, head), device_id_type=MESH)

    pl.semaphore_wait(barrier, count)

    def remote(src, dst, send, recv, device):
        return pltpu.make_async_remote_copy(
            src_ref=src,
            dst_ref=dst,
            send_sem=send,
            recv_sem=recv,
            device_id=device,
            device_id_type=MESH,
        )

    partner = (srv, other)
    piece = tok_dev // TOK_PIECES
    pair_tok = []
    for p in range(TOK_PIECES):
        rows = tok.at[head, pl.ds(p * piece, piece)]
        pair_tok.append(remote(rows, rows, pair_send.at[1 + p], pair_recv.at[1 + p], partner))
    pair_doc = remote(doc_hbm, docs.at[head], pair_send.at[0], pair_recv.at[0], partner)
    pair_doc.start()
    own_tok.wait()
    for copy in pair_tok:
        copy.start()
    for copy in wq_copies:
        copy.start()

    def doc_copy(by):
        return remote(
            docs.at[pl.ds(0, 2)],
            docs.at[pl.ds(2 * by, 2)],
            doc_send.at[by - 1],
            doc_recv.at[by - 1],
            (srv + by, head),
        )

    halves = (head, other)

    def kv_copy(by, turn, c):
        return remote(
            kv.at[0, c, halves[turn]],
            kv.at[by, c, halves[turn]],
            kv_send.at[by - 1, turn, c],
            kv_recv.at[by - 1, turn, c],
            (srv + by, head),
        )

    def kv_forward(turn, c):
        return remote(
            kv.at[2, c, halves[turn]],
            kv.at[1, c, halves[turn]],
            kv_send.at[0, turn, c],
            kv_recv.at[0, turn, c],
            (srv - 1, head),
        )

    sends_one = even & (srv + 1 < n)
    sends_two = srv + 2 < n
    forwards = odd & (srv >= 2)

    def project_kv(turn, first):
        half = halves[turn]
        if first:
            wkv_copies[0].wait()
        keys = jnp.dot(tok[half], wkv[0], preferred_element_type=jnp.float32)
        if first:
            wkv_copies[1].wait()
        values = jnp.dot(tok[half], wkv[1], preferred_element_type=jnp.float32)
        for c in range(kv_heads):
            cols = slice(c * HEAD, (c + 1) * HEAD)
            kv[0, c, half, :, :HEAD] = keys[:, cols].astype(jnp.bfloat16)
            kv[0, c, half, :, HEAD:] = jnp.transpose(values[:, cols]).astype(jnp.bfloat16)

            @pl.when(sends_two & even if turn else sends_two)
            def _():
                kv_copy(2, turn, c).start()

            @pl.when(sends_one)
            def _():
                kv_copy(1, turn, c).start()

    def project_q(block):
        rows = tok[:, :, block * depth : (block + 1) * depth].reshape(2 * tok_dev, depth)
        for j in range(q_blocks):
            part = jnp.dot(
                rows, wq[block, :, j * 256 : (j + 1) * 256], preferred_element_type=jnp.float32
            )
            if block:
                part = part + q_sum[j]
            if block + 1 < len(wq_copies):
                q_sum[j] = part
            else:
                q[2 * j] = part[:, :HEAD].astype(jnp.bfloat16)
                q[2 * j + 1] = part[:, HEAD:].astype(jnp.bfloat16)

    def forward(turn, c):
        @pl.when(forwards)
        def _():
            kv_copy(2, turn, c).wait_recv()
            kv_forward(turn, c).start()

    own_doc.wait()
    project_kv(0, True)
    pair_doc.wait_recv()
    for by in (1, 2):

        @pl.when(srv + by < n)
        def _(by=by):
            doc_copy(by).start()

    for copy in pair_tok:
        copy.wait_recv()
    project_kv(1, False)
    for block in range(len(wq_copies)):
        wq_copies[block].wait()
        project_q(block)
        if block % 2 == 0 and block // 2 < kv_heads:

            @pl.when(sends_two & odd)
            def _():
                kv_copy(2, 1, block // 2).start()

    for c in range(kv_heads):
        forward(0, c)

    def column(part):
        ids = docs[part].astype(jnp.float32)
        return jnp.transpose(jnp.broadcast_to(ids, (HEAD, HEAD)))

    def set_bias(block):
        for s in range(2):
            theirs = column(2 * block + s)
            for r in range(2):
                mine = docs[r].astype(jnp.float32)
                allowed = theirs == mine
                if block == 0:
                    keys = lax.broadcasted_iota(jnp.int32, (HEAD, HEAD), 0) + s * HEAD
                    queries = lax.broadcasted_iota(jnp.int32, (HEAD, HEAD), 1) + r * HEAD
                    allowed = allowed & (keys <= queries)
                bias[block, r, s * HEAD : (s + 1) * HEAD, :] = jnp.where(allowed, 0.0, MASKED)

    first_key = {0: (0, 0), 1: (0, 0), 2: (0, tok_dev)}
    last_key = {0: (tok_dev, 2 * tok_dev), 1: (2 * tok_dev,) * 2, 2: (2 * tok_dev,) * 2}

    def attend(block, c):
        keys = kv[block, c].reshape(2 * tok_dev, 2 * HEAD)[:, :HEAD]
        values = jnp.concatenate([kv[block, c, 0, :, HEAD:], kv[block, c, 1, :, HEAD:]], axis=1)
        values = jnp.concatenate([values, jnp.ones((ONES, 2 * tok_dev), jnp.bfloat16)], axis=0)
        for g in range(REPEAT):
            h = c * REPEAT + g
            for r in range(2):
                lo, hi = first_key[block][r], last_key[block][r]
                score = lax.dot_general(
                    keys[lo:hi],
                    q[h, r * tok_dev : (r + 1) * tok_dev],
                    (((1,), (1,)), ((), ())),
                    preferred_element_type=jnp.float32,
                )
                score = score + bias[block, r, lo:hi]
                high = jnp.max(score, axis=0, keepdims=True)
                if block:
                    before = top[h, r]
                    high = jnp.maximum(high, before)
                weight = jnp.exp2((score - high) * EXP2_SCALE).astype(jnp.bfloat16)
                part = jnp.dot(values[:, lo:hi], weight, preferred_element_type=jnp.float32)
                if block:
                    part = part + acc[h, r] * jnp.exp2((before - high) * EXP2_SCALE)
                acc[h, r] = part
                if block != 1:
                    top[h, r] = high

    identity = (
        lax.broadcasted_iota(jnp.int32, (tok_dev, tok_dev), 0)
        == lax.broadcasted_iota(jnp.int32, (tok_dev, tok_dev), 1)
    ).astype(jnp.bfloat16)

    def result(h, half):
        total = acc[h, half, HEAD : HEAD + 1]
        rounded = (acc[h, half, :HEAD] * (1.0 / total)).astype(jnp.bfloat16)
        return lax.dot_general(
            identity, rounded, (((1,), (1,)), ((), ())), preferred_element_type=jnp.float32
        ).astype(jnp.bfloat16)

    set_bias(0)
    for c in range(kv_heads):
        attend(0, c)
    for c in range(kv_heads):
        forward(1, c)

    @pl.when(srv >= 2)
    def _():
        doc_copy(2).wait_recv()
        set_bias(2)
        for c in range(kv_heads):

            @pl.when(even)
            def _():
                for turn in range(2):
                    kv_copy(2, turn, c).wait_recv()

            attend(2, c)

    @pl.when(srv >= 1)
    def _():
        doc_copy(1).wait_recv()
        set_bias(1)

    def out_copy(c):
        width = REPEAT * HEAD
        column_of = pl.multiple_of(head * kv_heads * width + c * width, width)
        return remote(
            stage.at[c],
            out_ref.at[:, pl.ds(column_of, width)],
            out_send.at[c],
            out_recv.at[c],
            partner,
        )

    for c in range(kv_heads):

        @pl.when(srv >= 1)
        def _():
            for turn in range(2):
                kv_copy(1, turn, c).wait_recv()
            attend(1, c)

        for g in range(REPEAT):
            h = c * REPEAT + g
            stage[c, :, g * HEAD : (g + 1) * HEAD] = result(h, other)
        out_copy(c).start()
        for g in range(REPEAT):
            h = c * REPEAT + g
            at = pl.multiple_of((head * kv_heads + c) * REPEAT * HEAD + g * HEAD, HEAD)
            out_ref[:, pl.ds(at, HEAD)] = result(h, head)

    for copy in pair_tok:
        copy.wait_send()
    pair_doc.wait_send()
    for by in (1, 2):

        @pl.when(srv + by < n)
        def _(by=by):
            doc_copy(by).wait_send()

    for turn in range(2):
        for c in range(kv_heads):

            @pl.when(sends_two)
            def _():
                kv_copy(2, turn, c).wait_send()

            @pl.when(sends_one)
            def _():
                kv_copy(1, turn, c).wait_send()

            @pl.when(forwards)
            def _():
                kv_forward(turn, c).wait_send()

    for c in range(kv_heads):
        out_copy(c).wait()


def on_device(n, tokens, doc_ids, w_query, w_key, value_weight):
    tok_dev, width = tokens.shape
    kv_heads = w_key.shape[1] // HEAD
    heads = w_query.shape[1] // HEAD
    q_blocks = heads // 2
    bf16, f32 = jnp.bfloat16, jnp.float32
    dma = pltpu.SemaphoreType.DMA
    return pl.pallas_call(
        functools.partial(kernel, n),
        out_shape=jax.ShapeDtypeStruct((tok_dev, 2 * heads * HEAD), bf16),
        in_specs=[pl.BlockSpec(memory_space=pltpu.HBM)] * 5,
        out_specs=pl.BlockSpec(memory_space=pltpu.VMEM),
        scratch_shapes=[
            pltpu.VMEM((2, tok_dev, width), bf16),
            pltpu.VMEM((2, width, kv_heads * HEAD), bf16),
            pltpu.VMEM((ROW_BLOCKS, width // ROW_BLOCKS, heads * HEAD), bf16),
            pltpu.VMEM((3, kv_heads, 2, tok_dev, 2 * HEAD), bf16),
            pltpu.VMEM((heads, 2 * tok_dev, HEAD), bf16),
            pltpu.VMEM((q_blocks, 2 * tok_dev, 256), f32),
            pltpu.VMEM((heads, 2, HEAD + ONES, tok_dev), f32),
            pltpu.VMEM((heads, 2, 1, tok_dev), f32),
            pltpu.VMEM((3, 2, 2 * tok_dev, tok_dev), f32),
            pltpu.VMEM((6, 1, tok_dev), jnp.int32),
            pltpu.VMEM((kv_heads, tok_dev, REPEAT * HEAD), bf16),
            dma,
            dma((2,)),
            dma((ROW_BLOCKS,)),
            dma,
            dma((1 + TOK_PIECES,)),
            dma((1 + TOK_PIECES,)),
            dma((2,)),
            dma((2,)),
            dma((2, 2, kv_heads)),
            dma((2, 2, kv_heads)),
            dma((kv_heads,)),
            dma((kv_heads,)),
        ],
        compiler_params=pltpu.CompilerParams(
            collective_id=0, has_side_effects=True, vmem_limit_bytes=53 * 1024 * 1024
        ),
    )(tokens, doc_ids.reshape(1, tok_dev), w_query, w_key, value_weight)


def solution(mesh):
    in_specs = (
        P(("srv", "head"), None),
        P(("srv", "head")),
        P(None, "head"),
        P(None, "head"),
        P(None, "head"),
    )
    return jax.shard_map(
        functools.partial(on_device, mesh.shape["srv"]),
        mesh=mesh,
        in_specs=in_specs,
        out_specs=P(("srv", "head"), None),
        check_vma=False,
    )
```
